512 devices in a mesh: clus: 128 (over y, x_hi, z), rows: 4 (over x_lo, core).
Axes of the slice: x: 4 (x_hi: 2, x_lo: 2; x = x_hi * 2 + x_lo), y: 8, z: 8, core: 2. Of those that a mesh axis runs over, the one named last changes fastest.
Arguments:
- right_sides: bfloat16 [256, 1024, 512], P('clus', 'rows'), may hold values from -6 to 6
- leaf_blocks: bfloat16 [256, 1024, 1024], P('clus', 'rows'), may hold values from -0.1875 to 0.1875
- basis_left: bfloat16 [8, 256, 1024, 128], P(None, 'clus', 'rows'), may hold values from -0.1875 to 0.1875
- basis_right: bfloat16 [8, 256, 1024, 128], P(None, 'clus', 'rows')
- block_ranks: int32 [510], replicated, may hold values from 32 to 128, as said below
Outputs:
- product: bfloat16 [256, 1024, 512], P('clus', 'rows')
The draws below stay inside these ranges and needn't reach their ends.
Inputs may be any that keep to these rules, and one draw needn't show every extreme that they name: `block_ranks`: every block's rank lies between 32 and 128; the top level's first block has rank 128.
All inputs are finite; a program needn't handle non-finite values.
Results may differ from the reference program's by a relative error of at most 0.0036.
Values may be sent and summed in bfloat16 or wider, within the bound.
No kernel may reach another device: no remote copies, remote signals or barrier semaphores. Data moves between devices by JAX's collectives and lax.ppermute only.
A program may use at most 64 MiB of HBM per device.

```python
import jax
import jax.numpy as jnp
from jax import lax

LEAF = 1024
RMAX = 128
RHS = 512
LEAVES = 256
LEVELS = 8
CLUSTERS = 510


def draw_basis_right(key, part):
    key = jax.random.fold_in(key, 11)
    shape = (LEVELS, LEAVES, LEAF, RMAX)
    values = jax.random.normal(key, shape, jnp.float32)
    level = jnp.arange(LEVELS, dtype=jnp.float32)
    scale = jnp.sqrt(2.0 ** (level + 1.0) / (LEAF * LEAVES))
    return (values * scale[:, None, None, None]).astype(jnp.bfloat16)


def draw_block_ranks(key, part):
    key = jax.random.fold_in(key, 23)
    drawn = jax.random.randint(key, (CLUSTERS,), RMAX // 4, RMAX + 1, dtype=jnp.int32)
    return drawn.at[0].set(RMAX)


def steps_of(own_key, shape, split, least, high):
    def one(position, shards_of):
        steps = jax.random.uniform(jax.random.fold_in(jax.random.fold_in(own_key, 6), position), (shards_of,), jnp.float32, least / len(split), high / len(split))
        return jnp.repeat(jnp.exp(steps), shape[position] // shards_of).reshape((-1,) + (1,) * (len(shape) - position - 1))

    factor_of = one(*split[0])
    for cut in split[1:]:
        factor_of = factor_of * one(*cut)
    return factor_of


def noise(stream_key, dims, deviation, limit, split=(), kind=jnp.bfloat16):
    entries = jax.random.normal(stream_key, dims, jnp.float32) * deviation
    if len(split) > 0:
        entries = steps_of(stream_key, dims, split, -0.22, 0.18) * entries
    return jnp.clip(entries, min=-limit, max=limit).astype(kind)


def setup_inputs(seed: int = 0) -> dict:
    keys = jax.random.split(jax.random.key(seed), 6)
    right_sides = noise(keys[0], (LEAVES, LEAF, RHS), 1.0, 6.0, ((0, 128), (1, 4)))
    leaf_blocks = noise(keys[1], (LEAVES, LEAF, LEAF), LEAF ** -0.5, 0.1875, ((0, 128), (1, 4)))
    basis_left = noise(keys[2], (LEVELS, LEAVES, LEAF, RMAX), (RMAX * LEVELS) ** -0.5, 0.1875, ((1, 128), (2, 4)))
    basis_right = draw_basis_right(jax.random.fold_in(keys[5], 71), 0)
    block_ranks = draw_block_ranks(jax.random.fold_in(keys[5], 71), 0)
    return {"right_sides": right_sides, "leaf_blocks": leaf_blocks, "basis_left": basis_left, "basis_right": basis_right, "block_ranks": block_ranks}


def leaf_product(pair):
    return jnp.dot(pair[0], pair[1], preferred_element_type=jnp.float32)


def reference(right_sides, leaf_blocks, basis_left, basis_right, block_ranks):
    accumulated = lax.map(leaf_product, (leaf_blocks, right_sides))
    columns = jnp.arange(RMAX, dtype=jnp.int32)
    for level in range(LEVELS):
        count = 2 ** (level + 1)
        group = LEAVES // count
        right_basis = basis_right[level].astype(jnp.float32).reshape(count, group * LEAF, RMAX)
        vectors = right_sides.astype(jnp.float32).reshape(count, group * LEAF, RHS)
        projection = jnp.einsum('cnj,cnh->cjh', right_basis, vectors)
        sibling = projection.reshape(count // 2, 2, RMAX, RHS)[:, ::-1].reshape(count, RMAX, RHS)
        sibling = sibling.astype(jnp.bfloat16)
        level_ranks = block_ranks[count - 2: 2 * count - 2]
        keep_rows = (columns[None, :] < level_ranks[:, None]).astype(jnp.bfloat16)
        coefficient = sibling * keep_rows[:, :, None]
        left_basis = basis_left[level].astype(jnp.float32).reshape(count, group * LEAF, RMAX)
        update = jnp.einsum('cnj,cjh->cnh', left_basis, coefficient.astype(jnp.float32))
        accumulated = accumulated + update.reshape(LEAVES, LEAF, RHS)
    return accumulated.astype(jnp.bfloat16)
```

```python
import functools

import jax
import jax.numpy as jnp
from jax import lax
from jax.experimental import pallas as pl
from jax.experimental.pallas import tpu as pltpu
from jax.sharding import Mesh, PartitionSpec as P

VMEM_BYTES = 48 * 1024 * 1024
F32 = jnp.float32
BF16 = jnp.bfloat16


def call(kernel, out_shape, in_specs, scratch=(), flops=0, moved=0):
    many = isinstance(out_shape, (list, tuple))
    whole = pl.BlockSpec(memory_space=pltpu.VMEM)
    return pl.pallas_call(
        kernel,
        out_shape=out_shape,
        in_specs=in_specs,
        out_specs=[whole] * len(out_shape) if many else whole,
        scratch_shapes=list(scratch),
        compiler_params=pltpu.CompilerParams(vmem_limit_bytes=VMEM_BYTES),
        cost_estimate=pl.CostEstimate(flops=flops, bytes_accessed=moved, transcendentals=0),
    )


SMEM = pl.BlockSpec(memory_space=pltpu.SMEM)
VMEM = pl.BlockSpec(memory_space=pltpu.VMEM)


def project_kernel(other, place, basis, sides, out):
    levels, leaves, rows, rank = basis.shape
    half = sides.shape[2] // 2
    core = place[1]
    column = pl.multiple_of((1 - core if other else core) * half, half)
    both = sides[:, :, pl.ds(column, half)]
    contract = (((0,), (0,)), ((), ()))
    for level in range(levels - 1):
        out[level] = lax.dot_general(
            basis[level].reshape(leaves * rows, rank),
            both.reshape(leaves * rows, half),
            contract,
            preferred_element_type=F32,
        )
    for leaf in range(leaves):
        out[levels - 1 + leaf] = lax.dot_general(
            basis[levels - 1, leaf], both[leaf], contract, preferred_element_type=F32
        )


def combine_kernel(mine, theirs, tiles, finest):
    upper = mine.shape[0] - finest.shape[0]
    slots, down, across = tiles.shape[:3]
    for level in range(upper):
        total = mine[level] + theirs[level]
        for col in range(across):
            part = total[:, col * 128 : (col + 1) * 128]
            tiles[level, :, col] = part.reshape(down, 8, 128).astype(BF16)
    for level in range(upper, slots):
        tiles[level] = jnp.zeros(tiles.shape[1:], BF16)
    finest[...] = mine[upper:] + theirs[upper:]


def tree_kernel(place, parts, out, total):
    count = total.shape[0]
    bits = count.bit_length() - 1
    depth = bits - 1 - place[3] // 32
    whole = parts[...].astype(F32)
    total[...] = whole[:, 0] + whole[:, 1]

    def swapped(bit):
        view = total[...].reshape(count >> (bit + 1), 2, 1 << bit, 8, 128)
        flipped = jnp.concatenate([view[:, 1:], view[:, :1]], axis=1)
        return flipped.reshape(count, 8, 128)

    for bit in range(bits):

        @pl.when(bit < depth)
        def _():
            total[...] = total[...] + swapped(bit)

        @pl.when(bit == depth)
        def _():
            total[...] = swapped(bit)

    rounded = total[...].astype(BF16)
    out[:, 0] = rounded
    out[:, 1] = rounded


def dense_kernel(place, blocks, own, by_core, by_chip, by_both, out):
    leaves, rows, _ = blocks.shape
    row = place[2]
    for leaf in range(leaves):
        total = None
        for step, sides in enumerate((own, by_core, by_chip, by_both)):
            column = pl.multiple_of(jnp.bitwise_xor(row, step) * rows, rows)
            term = jnp.dot(
                blocks[leaf, :, pl.ds(column, rows)], sides[leaf], preferred_element_type=F32
            )
            total = term if total is None else total + term
        out[leaf] = total


def update(place, ranks, tiles, finest, basis, dense, column, coef, store):
    levels, leaves, rows, rank = basis.shape
    upper = levels - 1
    half = finest.shape[2]
    across = half // 128
    position = place[0]

    def keep(shape, heap):
        return lax.broadcasted_iota(jnp.int32, shape, 0) < ranks[heap]

    for level in range(upper):
        heap = 2 ** (level + 1) - 2 + lax.shift_right_logical(position, upper - 1 - level)
        for col in range(across):
            part = tiles[level, :, col].astype(F32).reshape(rank, 128)
            part = jnp.where(keep(part.shape, heap), part, 0.0)
            coef[level * rank : (level + 1) * rank, col * 128 : (col + 1) * 128] = part.astype(BF16)
    for leaf in range(leaves):
        heap = 2**levels - 2 + leaves * position + leaf
        part = finest[leaves - 1 - leaf].astype(F32)
        part = jnp.where(keep(part.shape, heap), part, 0.0)
        coef[upper * rank : levels * rank, :] = part.astype(BF16)
        left = jnp.concatenate([basis[level, leaf] for level in range(levels)], axis=1)
        term = jnp.dot(left, coef[...], preferred_element_type=F32)
        store(leaf, (dense[leaf, :, pl.ds(column, half)] + term).astype(BF16))


def own_kernel(place, ranks, tiles, finest, basis, dense, out, coef):
    half = out.shape[2]
    column = pl.multiple_of(place[1] * half, half)

    def store(leaf, value):
        out[leaf] = value

    update(place, ranks, tiles, finest, basis, dense, column, coef, store)


def last_kernel(place, ranks, tiles, finest, basis, dense, ready, out, coef):
    half = ready.shape[2]
    mine = pl.multiple_of(place[1] * half, half)
    column = pl.multiple_of((1 - place[1]) * half, half)
    out[:, :, pl.ds(mine, half)] = ready[...]

    def store(leaf, value):
        out[leaf, :, pl.ds(column, half)] = value

    update(place, ranks, tiles, finest, basis, dense, column, coef, store)


def swap(block, axis):
    return lax.ppermute(block, axis, [(0, 1), (1, 0)])


def local(right_sides, leaf_blocks, basis_left, basis_right, block_ranks):
    leaves, rows, width = right_sides.shape
    levels, _, _, rank = basis_left.shape
    half = width // 2
    clusters = lax.axis_size("clus")
    owners = 2 * clusters
    position = lax.axis_index("clus")
    chip = lax.axis_index("chip")
    core = lax.axis_index("core")
    place = jnp.stack([position, core, 2 * chip + core, 2 * position + chip]).astype(jnp.int32)
    shape = jax.ShapeDtypeStruct
    slots = levels - 1 + leaves
    flops = 2 * levels * leaves * rows * rank * half

    def project(other):
        return call(
            functools.partial(project_kernel, other),
            shape((slots, rank, half), F32),
            [SMEM, VMEM, VMEM],
            flops=flops,
            moved=2 * (basis_right.size + right_sides.size) + 4 * slots * rank * half,
        )(place, basis_right, right_sides)

    sent = project(True)
    theirs = swap(sent, "core")
    mine = project(False)
    tiles, finest = call(
        combine_kernel,
        [shape((levels, rank // 8, half // 128, 8, 128), BF16), shape((leaves, rank, half), F32)],
        [VMEM, VMEM],
        moved=10 * slots * rank * half,
    )(mine, theirs)
    parts = lax.all_to_all(
        tiles.reshape(owners, 8, 128), ("clus", "chip"), split_axis=0, concat_axis=0, tiled=True
    )
    by_chip = swap(right_sides, "chip")
    by_core = swap(right_sides, "core")
    by_both = swap(by_chip, "core")
    finest = (finest + swap(finest, "chip")).astype(BF16)
    finest_other = swap(finest, "core")
    dense = call(
        dense_kernel,
        shape((leaves, rows, width), F32),
        [SMEM] + [VMEM] * 5,
        flops=2 * leaves * rows * leaf_blocks.shape[2] * width,
        moved=2 * leaf_blocks.size + 8 * right_sides.size + 4 * right_sides.size,
    )(place, leaf_blocks, right_sides, by_core, by_chip, by_both)
    coefs = call(
        tree_kernel,
        shape((clusters, 2, 8, 128), BF16),
        [SMEM, VMEM],
        scratch=[pltpu.VMEM((clusters, 8, 128), F32)],
        moved=4 * owners * 1024,
    )(place, parts.reshape(clusters, 2, 8, 128))
    coefs = lax.all_to_all(
        coefs.reshape(owners, 8, 128), ("clus", "chip"), split_axis=0, concat_axis=0, tiled=True
    ).reshape(tiles.shape)
    coefs_other = swap(coefs, "core")
    scratch = [pltpu.VMEM((levels * rank, half), BF16)]
    moved = 2 * (basis_left.size + coefs.size) + 4 * right_sides.size
    ready = call(
        own_kernel,
        shape((leaves, rows, half), BF16),
        [SMEM, SMEM] + [VMEM] * 4,
        scratch=scratch,
        flops=flops,
        moved=moved,
    )(place, block_ranks, coefs, finest, basis_left, dense)
    return call(
        last_kernel,
        shape((leaves, rows, width), BF16),
        [SMEM, SMEM] + [VMEM] * 5,
        scratch=scratch,
        flops=flops,
        moved=moved,
    )(place, block_ranks, coefs_other, finest_other, basis_left, dense, ready)


def solution(mesh):
    clusters = mesh.shape["clus"]
    fine = Mesh(mesh.devices.reshape(clusters, 2, 2), ("clus", "chip", "core"))
    rows = ("chip", "core")
    in_specs = (
        P("clus", rows, None),
        P("clus", rows, None),
        P(None, "clus", rows, None),
        P(None, "clus", rows, None),
        P(),
    )
    return jax.shard_map(
        local, mesh=fine, in_specs=in_specs, out_specs=P("clus", rows, None), check_vma=False
    )
```

```python
import functools

import jax
import jax.numpy as jnp
from jax import lax
from jax.experimental import pallas as pl
from jax.experimental.pallas import tpu as pltpu
from jax.sharding import Mesh, PartitionSpec as P

VMEM_BYTES = 48 * 1024 * 1024
F32 = jnp.float32
BF16 = jnp.bfloat16


def call(kernel, out_shape, in_specs, scratch=(), flops=0, moved=0):
    many = isinstance(out_shape, (list, tuple))
    whole = pl.BlockSpec(memory_space=pltpu.VMEM)
    return pl.pallas_call(
        kernel,
        out_shape=out_shape,
        in_specs=in_specs,
        out_specs=[whole] * len(out_shape) if many else whole,
        scratch_shapes=list(scratch),
        compiler_params=pltpu.CompilerParams(vmem_limit_bytes=VMEM_BYTES),
        cost_estimate=pl.CostEstimate(flops=flops, bytes_accessed=moved, transcendentals=0),
    )


SMEM = pl.BlockSpec(memory_space=pltpu.SMEM)
VMEM = pl.BlockSpec(memory_space=pltpu.VMEM)
ANY = pl.BlockSpec(memory_space=pl.ANY)


def project_kernel(other, place, basis, sides, out):
    levels, leaves, rows, rank = basis.shape
    half = sides.shape[2] // 2
    core = place[1]
    column = pl.multiple_of((1 - core if other else core) * half, half)
    both = sides[:, :, pl.ds(column, half)]
    contract = (((0,), (0,)), ((), ()))
    for level in range(levels - 1):
        out[level] = lax.dot_general(
            basis[level].reshape(leaves * rows, rank),
            both.reshape(leaves * rows, half),
            contract,
            preferred_element_type=F32,
        )
    for leaf in range(leaves):
        out[levels - 1 + leaf] = lax.dot_general(
            basis[levels - 1, leaf], both[leaf], contract, preferred_element_type=F32
        )


def combine_kernel(mine, theirs, tiles, finest):
    down, upper, across = tiles.shape[:3]
    for level in range(upper):
        total = mine[level] + theirs[level]
        for col in range(across):
            part = total[:, col * 128 : (col + 1) * 128]
            tiles[:, level, col] = part.reshape(down, 8, 128).astype(BF16)
    finest[...] = (mine[upper:] + theirs[upper:]).astype(BF16)


def ring_kernel(place, parts, *rest):
    out = rest[-1]
    high = place[3]
    bits = out.shape[0].bit_length() - 1
    total = [None] * bits
    for level in range(bits):
        for member in range(parts.shape[0]):
            part = parts[member, level].astype(F32)
            total[level] = part if total[level] is None else total[level] + part
    out[high] = jnp.zeros(out.shape[1:], F32)
    for step in range(1, out.shape[0]):
        out[jnp.bitwise_xor(high, step)] = total[bits - step.bit_length()]


def low_kernel(parts, sides, out, sides_out):
    sides_out[...] = sides[...]
    count, low = out.shape[:2]
    first = parts.shape[1] - low
    for level in range(low):
        part = [
            parts[2 * z, first + level].astype(F32) + parts[2 * z + 1, first + level].astype(F32)
            for z in range(count)
        ]
        distance = low - 1 - level
        size = 1 << distance
        sums = [sum(part[g * size + 1 : (g + 1) * size], part[g * size]) for g in range(count // size)]
        for z in range(count):
            out[z, level] = sums[(z >> distance) ^ 1].astype(BF16)


def back_kernel(place, high_parts, low, out):
    high = place[3]
    steps = high_parts.shape[0]
    bits = steps.bit_length() - 1
    for level in range(bits):
        first = 1 << (bits - 1 - level)
        total = high_parts[jnp.bitwise_xor(high, first)]
        for step in range(first + 1, 2 * first):
            total = total + high_parts[jnp.bitwise_xor(high, step)]
        rounded = total.astype(BF16)
        for member in range(out.shape[0]):
            out[member, level] = rounded
    for member in range(out.shape[0]):
        out[member, bits:] = low[member // 2]


def dense_kernel(place, blocks, own, by_core, by_chip, by_both, out):
    leaves, rows, _ = blocks.shape
    row = place[2]
    for leaf in range(leaves):
        total = None
        for step, sides in enumerate((own, by_core, by_chip, by_both)):
            column = pl.multiple_of(jnp.bitwise_xor(row, step) * rows, rows)
            term = jnp.dot(
                blocks[leaf, :, pl.ds(column, rows)], sides[leaf], preferred_element_type=F32
            )
            total = term if total is None else total + term
        out[leaf] = total


def gather_kernel(place, ranks, tiles, finest, finest_chip, dense, out):
    rank = tiles.shape[0] * 8
    upper, across = tiles.shape[1:3]
    position = place[0]

    def keep(shape, heap):
        return lax.broadcasted_iota(jnp.int32, shape, 0) < ranks[heap]

    for level in range(upper):
        heap = 2 ** (level + 1) - 2 + lax.shift_right_logical(position, upper - 1 - level)
        for col in range(across):
            part = tiles[:, level, col].astype(F32).reshape(rank, 128)
            part = jnp.where(keep(part.shape, heap), part, 0.0)
            row = (1 + level) * rank
            out[row : row + rank, col * 128 : (col + 1) * 128] = part.astype(BF16)
    for leaf in range(2):
        heap = 2 ** (upper + 1) - 2 + 2 * position + leaf
        part = finest[1 - leaf].astype(F32) + finest_chip[1 - leaf].astype(F32)
        part = jnp.where(keep(part.shape, heap), part, 0.0)
        row = leaf * (1 + upper) * rank
        out[row : row + rank, :] = part.astype(BF16)


def update(coef, basis, dense, column, store):
    levels, leaves, _, rank = basis.shape
    half = coef.shape[1]
    for leaf in range(leaves):
        order = list(range(levels - 1))
        order = order + [levels - 1] if leaf else [levels - 1] + order
        left = jnp.concatenate([basis[level, leaf] for level in order], axis=1)
        right = coef[leaf * rank : (leaf + levels) * rank, :]
        term = jnp.dot(left, right, preferred_element_type=F32)
        store(leaf, (dense[leaf, :, pl.ds(column, half)] + term).astype(BF16))


def own_kernel(place, coef, basis, dense, out):
    half = out.shape[2]
    column = pl.multiple_of(place[1] * half, half)

    def store(leaf, value):
        out[leaf] = value

    update(coef, basis, dense, column, store)


def last_kernel(place, coef, basis, dense, ready, out):
    half = ready.shape[2]
    mine = pl.multiple_of(place[1] * half, half)
    column = pl.multiple_of((1 - place[1]) * half, half)
    out[:, :, pl.ds(mine, half)] = ready[...]

    def store(leaf, value):
        out[leaf, :, pl.ds(column, half)] = value

    update(coef, basis, dense, column, store)


def swap(block, axis):
    return lax.ppermute(block, axis, [(0, 1), (1, 0)])


def local(right_sides, leaf_blocks, basis_left, basis_right, block_ranks):
    leaves, rows, width = right_sides.shape
    levels, _, _, rank = basis_left.shape
    half = width // 2
    upper = levels - 1
    ring = lax.axis_size("z")
    highs = lax.axis_size("high")
    low_levels = ring.bit_length() - 1
    owners = 2 * ring
    high = lax.axis_index("high")
    position = ring * high + lax.axis_index("z")
    chip = lax.axis_index("chip")
    core = lax.axis_index("core")
    place = jnp.stack([position, core, 2 * chip + core, high]).astype(jnp.int32)
    shape = jax.ShapeDtypeStruct
    slots = upper + leaves
    tile = (half // 128, 8, 128)
    flops = 2 * levels * leaves * rows * rank * half

    def project(other):
        return call(
            functools.partial(project_kernel, other),
            shape((slots, rank, half), F32),
            [SMEM, VMEM, VMEM],
            flops=flops,
            moved=2 * (basis_right.size + right_sides.size) + 4 * slots * rank * half,
        )(place, basis_right, right_sides)

    def exchange(block, axes):
        flat = block.reshape((block.shape[0], -1, 128))
        moved = lax.all_to_all(flat, axes, split_axis=0, concat_axis=0, tiled=True)
        return moved.reshape(block.shape)

    sent = project(True)
    theirs = swap(sent, "core")
    mine = project(False)
    tiles, finest = call(
        combine_kernel,
        [shape((owners, upper) + tile, BF16), shape((leaves, rank, half), BF16)],
        [VMEM, VMEM],
        moved=10 * slots * rank * half,
    )(mine, theirs)
    parts = exchange(tiles, ("z", "chip"))
    by_core = swap(right_sides, "core")
    finest_chip = swap(finest, "chip")
    to_high = call(
        ring_kernel,
        shape((highs,) + tile, F32),
        [SMEM, VMEM, ANY, ANY],
        moved=2 * parts.size,
    )(place, parts, finest_chip, by_core)
    low, sides_late = call(
        low_kernel,
        [shape((ring, low_levels) + tile, BF16), shape(right_sides.shape, BF16)],
        [VMEM, VMEM],
        moved=2 * parts.size + 4 * right_sides.size,
    )(parts, right_sides)
    from_high = exchange(to_high, ("high",))
    by_chip = swap(sides_late, "chip")
    by_both = swap(by_chip, "core")
    dense = call(
        dense_kernel,
        shape((leaves, rows, width), F32),
        [SMEM] + [VMEM] * 5,
        flops=2 * leaves * rows * leaf_blocks.shape[2] * width,
        moved=2 * leaf_blocks.size + 8 * right_sides.size + 4 * right_sides.size,
    )(place, leaf_blocks, right_sides, by_core, by_chip, by_both)
    coefs = call(
        back_kernel,
        shape(tiles.shape, BF16),
        [SMEM, VMEM, VMEM],
        moved=4 * parts.size,
    )(place, from_high, low)
    coefs = exchange(coefs, ("z", "chip"))
    coef = call(
        gather_kernel,
        shape((slots * rank, half), BF16),
        [SMEM, SMEM, VMEM, VMEM, VMEM, ANY],
        moved=4 * slots * rank * half,
    )(place, block_ranks, coefs, finest, finest_chip, dense)
    coef_other = swap(coef, "core")
    moved = 2 * (basis_left.size + coef.size) + 4 * right_sides.size
    ready = call(
        own_kernel,
        shape((leaves, rows, half), BF16),
        [SMEM] + [VMEM] * 3,
        flops=flops,
        moved=moved,
    )(place, coef, basis_left, dense)
    return call(
        last_kernel,
        shape((leaves, rows, width), BF16),
        [SMEM] + [VMEM] * 4,
        flops=flops,
        moved=moved,
    )(place, coef_other, basis_left, dense, ready)


def solution(mesh):
    clusters = mesh.shape["clus"]
    ring = 8
    fine = Mesh(
        mesh.devices.reshape(clusters // ring, ring, 2, 2), ("high", "z", "chip", "core")
    )
    places, rows = ("high", "z"), ("chip", "core")
    in_specs = (
        P(places, rows, None),
        P(places, rows, None),
        P(None, places, rows, None),
        P(None, places, rows, None),
        P(),
    )
    return jax.shard_map(
        local, mesh=fine, in_specs=in_specs, out_specs=P(places, rows, None), check_vma=False
    )
```

```python
import jax
import jax.numpy as jnp
from jax import lax
from jax.experimental import pallas as pl
from jax.experimental.pallas import tpu as pltpu
from jax.sharding import Mesh, PartitionSpec as P

VMEM_BYTES = 48 * 1024 * 1024
LONG = 10**10
F32 = jnp.float32
BF16 = jnp.bfloat16


def call(
    kernel, out_shape, in_specs, scratch=(), flops=0, moved=0, whole=None, aliases=None
):
    many = isinstance(out_shape, (list, tuple))
    whole = whole or VMEM
    return pl.pallas_call(
        kernel,
        out_shape=out_shape,
        in_specs=in_specs,
        out_specs=[whole] * len(out_shape) if many else whole,
        scratch_shapes=list(scratch),
        input_output_aliases=aliases or {},
        compiler_params=pltpu.CompilerParams(vmem_limit_bytes=VMEM_BYTES),
        cost_estimate=pl.CostEstimate(flops=flops, bytes_accessed=moved, transcendentals=0),
    )


SMEM = pl.BlockSpec(memory_space=pltpu.SMEM)
VMEM = pl.BlockSpec(memory_space=pltpu.VMEM)
ANY = pl.BlockSpec(memory_space=pl.ANY)


def projections(place, basis, sides):
    levels, leaves, rows, rank = basis.shape
    half = sides.shape[2] // 2
    both = sides[:, :, pl.ds(pl.multiple_of(place[1] * half, half), half)]
    contract = (((0,), (0,)), ((), ()))
    for level in range(levels - 1):
        yield lax.dot_general(
            basis[level].reshape(leaves * rows, rank),
            both.reshape(leaves * rows, half),
            contract,
            preferred_element_type=F32,
        )
    for leaf in range(leaves):
        yield lax.dot_general(
            basis[levels - 1, leaf], both[leaf], contract, preferred_element_type=F32
        )


def mine_kernel(place, basis, sides, out):
    for slot, value in enumerate(projections(place, basis, sides)):
        out[slot] = value


def theirs_kernel(place, basis, sides, mine, tiles, finest):
    down, upper, across = tiles.shape[:3]
    for slot, value in enumerate(projections(place, basis, sides)):
        total = mine[slot] + value
        if slot >= upper:
            finest[slot - upper] = total.astype(BF16)
            continue
        for col in range(across):
            part = total[:, col * 128 : (col + 1) * 128]
            tiles[:, slot, col] = part.reshape(down, 8, 128).astype(BF16)


def ring_kernel(place, parts, out):
    high = place[3]
    bits = out.shape[0].bit_length() - 1
    total = [None] * bits
    for level in range(bits):
        for member in range(parts.shape[0]):
            part = parts[member, level].astype(F32)
            total[level] = part if total[level] is None else total[level] + part
    out[high] = jnp.zeros(out.shape[1:], F32)
    for step in range(1, out.shape[0]):
        out[jnp.bitwise_xor(high, step)] = total[bits - step.bit_length()]


def low_kernel(parts, sides, finest, out, sides_out, finest_out):
    sides_out[...] = sides[...]
    finest_out[...] = finest[...]
    count, low = out.shape[:2]
    first = parts.shape[1] - low
    for level in range(low):
        part = [
            parts[2 * z, first + level].astype(F32) + parts[2 * z + 1, first + level].astype(F32)
            for z in range(count)
        ]
        distance = low - 1 - level
        size = 1 << distance
        sums = [sum(part[g * size + 1 : (g + 1) * size], part[g * size]) for g in range(count // size)]
        for z in range(count):
            out[z, level] = sums[(z >> distance) ^ 1].astype(BF16)


def back_kernel(place, high_parts, low, finest_chip, out):
    high = place[3]
    steps = high_parts.shape[0]
    bits = steps.bit_length() - 1
    for level in range(bits):
        first = 1 << (bits - 1 - level)
        total = high_parts[jnp.bitwise_xor(high, first)]
        for step in range(first + 1, 2 * first):
            total = total + high_parts[jnp.bitwise_xor(high, step)]
        rounded = total.astype(BF16)
        for member in range(out.shape[0]):
            out[member, level] = rounded
    for member in range(out.shape[0]):
        out[member, bits:] = low[member // 2]


def dense_kernel(place, blocks, own, by_core, by_chip, by_both, out):
    leaves, rows, _ = blocks.shape
    row = place[2]
    for leaf in range(leaves):
        total = None
        for step, sides in enumerate((own, by_core, by_chip, by_both)):
            column = pl.multiple_of(jnp.bitwise_xor(row, step) * rows, rows)
            term = jnp.dot(
                blocks[leaf, :, pl.ds(column, rows)], sides[leaf], preferred_element_type=F32
            )
            total = term if total is None else total + term
        out[leaf] = total


def gather_kernel(place, ranks, tiles, finest, finest_chip, dense, out):
    rank = tiles.shape[0] * 8
    upper, across = tiles.shape[1:3]
    position = place[0]

    def keep(shape, heap):
        return lax.broadcasted_iota(jnp.int32, shape, 0) < ranks[heap]

    for level in range(upper):
        heap = 2 ** (level + 1) - 2 + lax.shift_right_logical(position, upper - 1 - level)
        for col in range(across):
            part = tiles[:, level, col].astype(F32).reshape(rank, 128)
            part = jnp.where(keep(part.shape, heap), part, 0.0)
            row = (1 + level) * rank
            out[row : row + rank, col * 128 : (col + 1) * 128] = part.astype(BF16)
    for leaf in range(2):
        heap = 2 ** (upper + 1) - 2 + 2 * position + leaf
        part = finest[1 - leaf].astype(F32) + finest_chip[1 - leaf].astype(F32)
        part = jnp.where(keep(part.shape, heap), part, 0.0)
        row = leaf * (1 + upper) * rank
        out[row : row + rank, :] = part.astype(BF16)


def update(coef, basis, dense, column, store):
    levels, leaves, _, rank = basis.shape
    half = coef.shape[1]
    for leaf in range(leaves):
        order = list(range(levels - 1))
        order = order + [levels - 1] if leaf else [levels - 1] + order
        left = jnp.concatenate([basis[level, leaf] for level in order], axis=1)
        right = coef[leaf * rank : (leaf + levels) * rank, :]
        term = jnp.dot(left, right, preferred_element_type=F32)
        store(leaf, (dense[leaf, :, pl.ds(column, half)] + term).astype(BF16))


def own_kernel(place, coef, basis, dense, out, held, sems):
    half = held.shape[2]
    place_half(place[1], coef, basis, dense, out, held, sems, half)


def last_kernel(place, coef, basis, dense, begun, out, held, sems):
    half = held.shape[2]
    place_half(1 - place[1], coef, basis, dense, out, held, sems, half)


def place_half(index, coef, basis, dense, out, held, sems, half):
    column = pl.multiple_of(index * half, half)
    copies = []

    def store(leaf, value):
        held[leaf] = value
        copies.append(
            pltpu.make_async_copy(
                held.at[leaf], out.at[leaf, :, pl.ds(column, half)], sems.at[leaf]
            )
        )
        copies[-1].start()

    update(coef, basis, dense, column, store)
    for copy in copies:
        copy.wait()


def swap(block, axis):
    return lax.ppermute(block, axis, [(0, 1), (1, 0)])


def local(right_sides, leaf_blocks, basis_left, basis_right, block_ranks):
    leaves, rows, width = right_sides.shape
    levels, _, _, rank = basis_left.shape
    half = width // 2
    upper = levels - 1
    ring = lax.axis_size("z")
    highs = lax.axis_size("high")
    low_levels = ring.bit_length() - 1
    owners = 2 * ring
    high = lax.axis_index("high")
    position = ring * high + lax.axis_index("z")
    chip = lax.axis_index("chip")
    core = lax.axis_index("core")
    place = jnp.stack([position, core, 2 * chip + core, high]).astype(jnp.int32)
    shape = jax.ShapeDtypeStruct
    slots = upper + leaves
    tile = (half // 128, 8, 128)
    flops = 2 * levels * leaves * rows * rank * half

    def exchange(block, axes):
        flat = block.reshape((block.shape[0], -1, 128))
        moved = lax.all_to_all(flat, axes, split_axis=0, concat_axis=0, tiled=True)
        return moved.reshape(block.shape)

    basis_core = swap(basis_right, "core")
    by_core = swap(right_sides, "core")
    moved = 2 * (basis_right.size + right_sides.size) + 4 * slots * rank * half
    mine = call(
        mine_kernel,
        shape((slots, rank, half), F32),
        [SMEM, VMEM, VMEM],
        flops=flops,
        moved=moved,
    )(place, basis_right, right_sides)
    tiles, finest = call(
        theirs_kernel,
        [shape((owners, upper) + tile, BF16), shape((leaves, rank, half), BF16)],
        [SMEM, VMEM, VMEM, VMEM],
        flops=flops,
        moved=2 * moved,
    )(place, basis_core, by_core, mine)
    parts = exchange(tiles, ("z", "chip"))
    to_high = call(
        ring_kernel, shape((highs,) + tile, F32), [SMEM, VMEM], moved=2 * parts.size
    )(place, parts)
    low, sides_late, finest_late = call(
        low_kernel,
        [
            shape((ring, low_levels) + tile, BF16),
            shape(right_sides.shape, BF16),
            shape(finest.shape, BF16),
        ],
        [VMEM, VMEM, VMEM],
        moved=2 * parts.size + 4 * right_sides.size,
    )(parts, right_sides, finest)
    from_high = exchange(to_high, ("high",))
    by_chip = swap(sides_late, "chip")
    finest_chip = swap(finest_late, "chip")
    by_both = swap(by_chip, "core")
    dense = call(
        dense_kernel,
        shape((leaves, rows, width), F32),
        [SMEM] + [VMEM] * 5,
        flops=2 * leaves * rows * leaf_blocks.shape[2] * width,
        moved=2 * leaf_blocks.size + 8 * right_sides.size + 4 * right_sides.size,
    )(place, leaf_blocks, right_sides, by_core, by_chip, by_both)
    coefs = call(
        back_kernel,
        shape(tiles.shape, BF16),
        [SMEM, VMEM, VMEM, VMEM],
        flops=LONG,
        moved=4 * parts.size,
    )(place, from_high, low, finest_chip)
    coefs = exchange(coefs, ("z", "chip"))
    coef = call(
        gather_kernel,
        shape((slots * rank, half), BF16),
        [SMEM, SMEM, VMEM, VMEM, VMEM, ANY],
        moved=4 * slots * rank * half,
    )(place, block_ranks, coefs, finest, finest_chip, dense)
    coef_other = swap(coef, "core")
    held = [pltpu.VMEM((leaves, rows, half), BF16), pltpu.SemaphoreType.DMA((leaves,))]
    moved = 2 * (basis_left.size + coef.size) + 4 * right_sides.size
    begun = call(
        own_kernel,
        shape((leaves, rows, width), BF16),
        [SMEM] + [VMEM] * 3,
        scratch=held,
        whole=ANY,
        flops=flops,
        moved=moved,
    )(place, coef, basis_left, dense)
    return call(
        last_kernel,
        shape((leaves, rows, width), BF16),
        [SMEM] + [VMEM] * 3 + [ANY],
        scratch=held,
        whole=ANY,
        aliases={4: 0},
        flops=flops,
        moved=moved,
    )(place, coef_other, basis_left, dense, begun)


def solution(mesh):
    clusters = mesh.shape["clus"]
    ring = 8
    fine = Mesh(
        mesh.devices.reshape(clusters // ring, ring, 2, 2), ("high", "z", "chip", "core")
    )
    places, rows = ("high", "z"), ("chip", "core")
    in_specs = (
        P(places, rows, None),
        P(places, rows, None),
        P(None, places, rows, None),
        P(None, places, rows, None),
        P(),
    )
    return jax.shard_map(
        local, mesh=fine, in_specs=in_specs, out_specs=P(places, rows, None), check_vma=False
    )
```

```python
import jax
import jax.numpy as jnp
from jax import lax
from jax.experimental import pallas as pl
from jax.experimental.pallas import tpu as pltpu
from jax.sharding import Mesh, PartitionSpec as P

VMEM_BYTES = 48 * 1024 * 1024
LONG = 10**10
F32 = jnp.float32
BF16 = jnp.bfloat16


def call(
    kernel, out_shape, in_specs, scratch=(), flops=0, moved=0, whole=None, aliases=None
):
    many = isinstance(out_shape, (list, tuple))
    whole = whole or VMEM
    return pl.pallas_call(
        kernel,
        out_shape=out_shape,
        in_specs=in_specs,
        out_specs=[whole] * len(out_shape) if many else whole,
        scratch_shapes=list(scratch),
        input_output_aliases=aliases or {},
        compiler_params=pltpu.CompilerParams(vmem_limit_bytes=VMEM_BYTES),
        cost_estimate=pl.CostEstimate(flops=flops, bytes_accessed=moved, transcendentals=0),
    )


SMEM = pl.BlockSpec(memory_space=pltpu.SMEM)
VMEM = pl.BlockSpec(memory_space=pltpu.VMEM)
ANY = pl.BlockSpec(memory_space=pl.ANY)


def projections(place, basis, sides):
    levels, leaves, rows, rank = basis.shape
    half = sides.shape[2] // 2
    both = sides[:, :, pl.ds(pl.multiple_of(place[1] * half, half), half)]
    contract = (((0,), (0,)), ((), ()))
    for level in range(levels - 1):
        yield lax.dot_general(
            basis[level].reshape(leaves * rows, rank),
            both.reshape(leaves * rows, half),
            contract,
            preferred_element_type=F32,
        )
    for leaf in range(leaves):
        yield lax.dot_general(
            basis[levels - 1, leaf], both[leaf], contract, preferred_element_type=F32
        )


def mine_kernel(place, basis, sides, out):
    for slot, value in enumerate(projections(place, basis, sides)):
        out[slot] = value


def theirs_kernel(place, basis, sides, mine, wide, near):
    down, wide_levels, across = wide.shape[:3]
    for slot, value in enumerate(projections(place, basis, sides)):
        total = mine[slot] + value
        if slot >= wide_levels:
            near[slot - wide_levels] = total.astype(BF16)
            continue
        for col in range(across):
            part = total[:, col * 128 : (col + 1) * 128]
            wide[:, slot, col] = part.reshape(down, 8, 128).astype(BF16)


def ring_kernel(place, parts, sides, out, sides_out):
    sides_out[...] = sides[...]
    high = place[3]
    bits = out.shape[0].bit_length() - 1
    total = [None] * bits
    for level in range(bits):
        for member in range(parts.shape[0]):
            part = parts[member, level].astype(F32)
            total[level] = part if total[level] is None else total[level] + part
    out[high] = jnp.zeros(out.shape[1:], F32)
    for step in range(1, out.shape[0]):
        out[jnp.bitwise_xor(high, step)] = total[bits - step.bit_length()]


def back_kernel(place, high_parts, parts, near_7, out):
    high = place[3]
    steps = high_parts.shape[0]
    bits = steps.bit_length() - 1
    members = out.shape[0]
    for level in range(bits):
        first = 1 << (bits - 1 - level)
        total = high_parts[jnp.bitwise_xor(high, first)]
        for step in range(first + 1, 2 * first):
            total = total + high_parts[jnp.bitwise_xor(high, step)]
        rounded = total.astype(BF16)
        for member in range(members):
            out[member, level] = rounded
    for side in range(2):
        first = (1 - side) * members // 2
        total = parts[first, bits].astype(F32)
        for member in range(first + 1, first + members // 2):
            total = total + parts[member, bits].astype(F32)
        rounded = total.astype(BF16)
        for member in range(side * members // 2, (side + 1) * members // 2):
            out[member, bits] = rounded


def dense_kernel(place, blocks, own, by_core, by_chip, by_both, out):
    leaves, rows, _ = blocks.shape
    row = place[2]
    for leaf in range(leaves):
        total = None
        for step, sides in enumerate((own, by_core, by_chip, by_both)):
            column = pl.multiple_of(jnp.bitwise_xor(row, step) * rows, rows)
            term = jnp.dot(
                blocks[leaf, :, pl.ds(column, rows)], sides[leaf], preferred_element_type=F32
            )
            total = term if total is None else total + term
        out[leaf] = total


def gather_kernel(place, ranks, wide, near_6, near_7, near, dense, out):
    rank = wide.shape[0] * 8
    wide_levels, across = wide.shape[1:3]
    upper = wide_levels + 2
    position = place[0]

    def put(row, column, value, heap):
        kept = lax.broadcasted_iota(jnp.int32, value.shape, 0) < ranks[heap]
        value = jnp.where(kept, value.astype(F32), 0.0).astype(BF16)
        out[row : row + rank, column : column + value.shape[1]] = value

    for level in range(upper):
        heap = 2 ** (level + 1) - 2 + lax.shift_right_logical(position, upper - 1 - level)
        row = (1 + level) * rank
        if level < wide_levels:
            for col in range(across):
                put(row, col * 128, wide[:, level, col].astype(F32).reshape(rank, 128), heap)
        else:
            put(row, 0, near_6[...] if level == wide_levels else near_7[1], heap)
    for leaf in range(2):
        heap = 2 ** (upper + 1) - 2 + 2 * position + leaf
        put(leaf * (1 + upper) * rank, 0, near[3 - leaf], heap)


def update(coef, basis, dense, column, store):
    levels, leaves, _, rank = basis.shape
    half = coef.shape[1]
    for leaf in range(leaves):
        order = list(range(levels - 1))
        order = order + [levels - 1] if leaf else [levels - 1] + order
        left = jnp.concatenate([basis[level, leaf] for level in order], axis=1)
        right = coef[leaf * rank : (leaf + levels) * rank, :]
        term = jnp.dot(left, right, preferred_element_type=F32)
        store(leaf, (dense[leaf, :, pl.ds(column, half)] + term).astype(BF16))


def own_kernel(place, coef, basis, dense, out, held, sems):
    half = held.shape[2]
    place_half(place[1], coef, basis, dense, out, held, sems, half)


def last_kernel(place, coef, basis, dense, begun, out, held, sems):
    half = held.shape[2]
    place_half(1 - place[1], coef, basis, dense, out, held, sems, half)


def place_half(index, coef, basis, dense, out, held, sems, half):
    column = pl.multiple_of(index * half, half)
    copies = []

    def store(leaf, value):
        held[leaf] = value
        copies.append(
            pltpu.make_async_copy(
                held.at[leaf], out.at[leaf, :, pl.ds(column, half)], sems.at[leaf]
            )
        )
        copies[-1].start()

    update(coef, basis, dense, column, store)
    for copy in copies:
        copy.wait()


def swap(block, axis, bit=1):
    return lax.ppermute(block, axis, [(i, i ^ bit) for i in range(lax.axis_size(axis))])


def local(right_sides, leaf_blocks, basis_left, basis_right, block_ranks):
    leaves, rows, width = right_sides.shape
    levels, _, _, rank = basis_left.shape
    half = width // 2
    upper = levels - 1
    ring = lax.axis_size("z")
    highs = lax.axis_size("high")
    wide_levels = levels - 3
    owners = 2 * ring
    high = lax.axis_index("high")
    position = ring * high + lax.axis_index("z")
    chip = lax.axis_index("chip")
    core = lax.axis_index("core")
    place = jnp.stack([position, core, 2 * chip + core, high]).astype(jnp.int32)
    shape = jax.ShapeDtypeStruct
    slots = upper + leaves
    tile = (half // 128, 8, 128)
    flops = 2 * levels * leaves * rows * rank * half

    def exchange(block, axes):
        flat = block.reshape((block.shape[0], -1, 128))
        moved = lax.all_to_all(flat, axes, split_axis=0, concat_axis=0, tiled=True)
        return moved.reshape(block.shape)

    basis_core = swap(basis_right, "core")
    by_core = swap(right_sides, "core")
    moved = 2 * (basis_right.size + right_sides.size) + 4 * slots * rank * half
    mine = call(
        mine_kernel,
        shape((slots, rank, half), F32),
        [SMEM, VMEM, VMEM],
        flops=flops,
        moved=moved,
    )(place, basis_right, right_sides)
    wide_shape = shape((owners, wide_levels) + tile, BF16)
    near_shape = (slots - wide_levels, rank, half)
    wide, near = call(
        theirs_kernel,
        [wide_shape, shape(near_shape, BF16)],
        [SMEM, VMEM, VMEM, VMEM],
        flops=flops,
        moved=2 * moved,
    )(place, basis_core, by_core, mine)
    wide = exchange(wide, ("z", "chip"))
    near = (near.astype(F32) + swap(near, "chip").astype(F32)).astype(BF16)
    near_7 = swap(near[:2], "z", 1)
    near_6 = swap((near[0].astype(F32) + near_7[0].astype(F32)).astype(BF16), "z", 2)
    to_high, sides_late = call(
        ring_kernel,
        [shape((highs,) + tile, F32), shape(right_sides.shape, BF16)],
        [SMEM, VMEM, VMEM],
        flops=LONG,
        moved=2 * wide.size,
    )(place, wide, right_sides)
    from_high = exchange(to_high, ("high",))
    by_chip = swap(sides_late, "chip")
    by_both = swap(by_chip, "core")
    wide = call(
        back_kernel,
        wide_shape,
        [SMEM, VMEM, VMEM, VMEM],
        flops=LONG,
        moved=4 * wide.size,
    )(place, from_high, wide, near_7)
    wide = exchange(wide, ("z", "chip"))
    dense = call(
        dense_kernel,
        shape((leaves, rows, width), F32),
        [SMEM] + [VMEM] * 5,
        flops=2 * leaves * rows * leaf_blocks.shape[2] * width,
        moved=2 * leaf_blocks.size + 12 * right_sides.size,
    )(place, leaf_blocks, right_sides, by_core, by_chip, by_both)
    coef = call(
        gather_kernel,
        shape((slots * rank, half), BF16),
        [SMEM, SMEM] + [VMEM] * 4 + [ANY],
        moved=4 * slots * rank * half,
    )(place, block_ranks, wide, near_6, near_7, near, dense)
    coef_other = swap(coef, "core")
    held = [pltpu.VMEM((leaves, rows, half), BF16), pltpu.SemaphoreType.DMA((leaves,))]
    moved = 2 * (basis_left.size + coef.size) + 4 * right_sides.size
    begun = call(
        own_kernel,
        shape((leaves, rows, width), BF16),
        [SMEM] + [VMEM] * 3,
        scratch=held,
        whole=ANY,
        flops=flops,
        moved=moved,
    )(place, coef, basis_left, dense)
    return call(
        last_kernel,
        shape((leaves, rows, width), BF16),
        [SMEM] + [VMEM] * 3 + [ANY],
        scratch=held,
        whole=ANY,
        aliases={4: 0},
        flops=flops,
        moved=moved,
    )(place, coef_other, basis_left, dense, begun)


def solution(mesh):
    clusters = mesh.shape["clus"]
    ring = 8
    fine = Mesh(
        mesh.devices.reshape(clusters // ring, ring, 2, 2), ("high", "z", "chip", "core")
    )
    places, rows = ("high", "z"), ("chip", "core")
    in_specs = (
        P(places, rows, None),
        P(places, rows, None),
        P(None, places, rows, None),
        P(None, places, rows, None),
        P(),
    )
    return jax.shard_map(
        local, mesh=fine, in_specs=in_specs, out_specs=P(places, rows, None), check_vma=False
    )
```

```python
import jax
import jax.numpy as jnp
from jax import lax
from jax.experimental import pallas as pl
from jax.experimental.pallas import tpu as pltpu
from jax.sharding import Mesh, PartitionSpec as P

VMEM_BYTES = 48 * 1024 * 1024
LONG = 20 * 10**8
LONG2 = 20 * 10**8
LONG3 = 30 * 10**8
F32 = jnp.float32
BF16 = jnp.bfloat16


def call(
    kernel, out_shape, in_specs, scratch=(), flops=0, moved=0, whole=None, aliases=None
):
    many = isinstance(out_shape, (list, tuple))
    whole = whole or VMEM
    return pl.pallas_call(
        kernel,
        out_shape=out_shape,
        in_specs=in_specs,
        out_specs=[whole] * len(out_shape) if many else whole,
        scratch_shapes=list(scratch),
        input_output_aliases=aliases or {},
        compiler_params=pltpu.CompilerParams(vmem_limit_bytes=VMEM_BYTES),
        cost_estimate=pl.CostEstimate(flops=flops, bytes_accessed=moved, transcendentals=0),
    )


SMEM = pl.BlockSpec(memory_space=pltpu.SMEM)
VMEM = pl.BlockSpec(memory_space=pltpu.VMEM)
ANY = pl.BlockSpec(memory_space=pl.ANY)


def place():
    high, chip, core = (lax.axis_index(axis) for axis in ("high", "chip", "core"))
    return lax.axis_size("z") * high + lax.axis_index("z"), core, 2 * chip + core, high


def projections( basis, sides):
    levels, leaves, rows, rank = basis.shape
    half = sides.shape[2] // 2
    both = sides[:, :, pl.ds(pl.multiple_of(place()[1] * half, half), half)]
    contract = (((0,), (0,)), ((), ()))
    for level in range(levels - 1):
        yield lax.dot_general(
            basis[level].reshape(leaves * rows, rank),
            both.reshape(leaves * rows, half),
            contract,
            preferred_element_type=F32,
        )
    for leaf in range(leaves):
        yield lax.dot_general(
            basis[levels - 1, leaf], both[leaf], contract, preferred_element_type=F32
        )


def mine_kernel(basis, sides, out):
    for slot, value in enumerate(projections(basis, sides)):
        out[slot] = value


def theirs_kernel(basis, sides, mine, wide, near):
    down, wide_levels, across = wide.shape[:3]
    for slot, value in enumerate(projections(basis, sides)):
        total = mine[slot] + value
        if slot >= wide_levels:
            near[slot - wide_levels] = total.astype(BF16)
            continue
        for col in range(across):
            part = total[:, col * 128 : (col + 1) * 128]
            wide[:, slot, col] = part.reshape(down, 8, 128).astype(BF16)


def ring_kernel(parts, out):
    high = place()[3]
    bits = out.shape[0].bit_length() - 1
    total = [None] * bits
    for level in range(bits):
        for member in range(parts.shape[0]):
            part = parts[member, level].astype(F32)
            total[level] = part if total[level] is None else total[level] + part
    out[high] = jnp.zeros(out.shape[1:], F32)
    for step in range(1, out.shape[0]):
        out[jnp.bitwise_xor(high, step)] = total[bits - step.bit_length()]


def back_kernel(high_parts, parts, near_7, out):
    high = place()[3]
    steps = high_parts.shape[0]
    bits = steps.bit_length() - 1
    members = out.shape[0]
    for level in range(bits):
        first = 1 << (bits - 1 - level)
        total = high_parts[jnp.bitwise_xor(high, first)]
        for step in range(first + 1, 2 * first):
            total = total + high_parts[jnp.bitwise_xor(high, step)]
        rounded = total.astype(BF16)
        for member in range(members):
            out[member, level] = rounded
    for side in range(2):
        first = (1 - side) * members // 2
        total = parts[first, bits].astype(F32)
        for member in range(first + 1, first + members // 2):
            total = total + parts[member, bits].astype(F32)
        rounded = total.astype(BF16)
        for member in range(side * members // 2, (side + 1) * members // 2):
            out[member, bits] = rounded


def dense_kernel(ranks, blocks, own, by_core, by_chip, by_both, basis, out, left):
    leaves, rows, _ = blocks.shape
    levels, _, _, rank = basis.shape
    position, _, row, _ = place()
    for leaf in range(leaves):
        total = None
        for step, sides in enumerate((own, by_core, by_chip, by_both)):
            column = pl.multiple_of(jnp.bitwise_xor(row, step) * rows, rows)
            term = jnp.dot(
                blocks[leaf, :, pl.ds(column, rows)], sides[leaf], preferred_element_type=F32
            )
            total = term if total is None else total + term
        out[leaf] = total
    columns = lax.broadcasted_iota(jnp.int32, (rows, rank), 1)
    for level in range(levels):
        for leaf in range(leaves):
            if level < levels - 1:
                heap = 2 ** (level + 1) - 2 + lax.shift_right_logical(position, levels - 2 - level)
                slot = level + 1 - leaf
            else:
                heap = 2**levels - 2 + leaves * position + leaf
                slot = level * leaf
            kept = jnp.where(columns < ranks[heap], basis[level, leaf].astype(F32), 0.0)
            left[leaf, :, slot * rank : (slot + 1) * rank] = kept.astype(BF16)


def gather_kernel(wide, near_6, near_7, near, late, out):
    rank = wide.shape[0] * 8
    wide_levels, across = wide.shape[1:3]
    for level in range(wide_levels):
        for col in range(across):
            part = wide[:, level, col].astype(F32).reshape(rank, 128).astype(BF16)
            out[(1 + level) * rank : (2 + level) * rank, col * 128 : (col + 1) * 128] = part
    row = (1 + wide_levels) * rank
    out[:rank] = near[3]
    for part in (near_6[...], near_7[1], near[2]):
        out[row : row + rank] = part
        row += rank


def update(coef, left, dense, column, store):
    leaves, _, depth = left.shape
    half = coef.shape[1]
    rank = coef.shape[0] - depth
    for leaf in range(leaves):
        term = jnp.dot(
            left[leaf], coef[leaf * rank : leaf * rank + depth], preferred_element_type=F32
        )
        store(leaf, (dense[leaf, :, pl.ds(column, half)] + term).astype(BF16))


def own_kernel(coef, left, dense, out, held, sems):
    half = held.shape[2]
    place_half(place()[1], coef, left, dense, out, held, sems, half)


def last_kernel(coef, left, dense, begun, out, held, sems):
    half = held.shape[2]
    place_half(1 - place()[1], coef, left, dense, out, held, sems, half)


def place_half(index, coef, left, dense, out, held, sems, half):
    column = pl.multiple_of(index * half, half)
    copies = []

    def store(leaf, value):
        held[leaf] = value
        copies.append(
            pltpu.make_async_copy(
                held.at[leaf], out.at[leaf, :, pl.ds(column, half)], sems.at[leaf]
            )
        )
        copies[-1].start()

    update(coef, left, dense, column, store)
    for copy in copies:
        copy.wait()


def swap(block, axis, bit=1):
    return lax.ppermute(block, axis, [(i, i ^ bit) for i in range(lax.axis_size(axis))])


def local(right_sides, leaf_blocks, basis_left, basis_right, block_ranks):
    leaves, rows, width = right_sides.shape
    levels, _, _, rank = basis_left.shape
    half = width // 2
    upper = levels - 1
    ring = lax.axis_size("z")
    highs = lax.axis_size("high")
    wide_levels = levels - 3
    owners = 2 * ring
    shape = jax.ShapeDtypeStruct
    slots = upper + leaves
    tile = (half // 128, 8, 128)
    flops = 2 * levels * leaves * rows * rank * half

    def exchange(block, axes):
        flat = block.reshape((block.shape[0], -1, 128))
        moved = lax.all_to_all(flat, axes, split_axis=0, concat_axis=0, tiled=True)
        return moved.reshape(block.shape)

    basis_core = swap(basis_right, "core")
    by_core = swap(right_sides, "core")
    moved = 2 * (basis_right.size + right_sides.size) + 4 * slots * rank * half
    mine = call(
        mine_kernel,
        shape((slots, rank, half), F32),
        [VMEM, VMEM],
        flops=flops,
        moved=moved,
    )(basis_right, right_sides)
    wide_shape = shape((owners, wide_levels) + tile, BF16)
    near_shape = (slots - wide_levels, rank, half)
    wide, near = call(
        theirs_kernel,
        [wide_shape, shape(near_shape, BF16)],
        [VMEM, VMEM, VMEM],
        flops=flops,
        moved=2 * moved,
    )(basis_core, by_core, mine)
    wide = exchange(wide, ("z", "chip"))
    near = (near.astype(F32) + swap(near, "chip").astype(F32)).astype(BF16)
    near_7 = swap(near[:2], "z", 1)
    near_6 = swap((near[0].astype(F32) + near_7[0].astype(F32)).astype(BF16), "z", 2)
    to_high = call(
        ring_kernel,
        shape((highs,) + tile, F32),
        [VMEM],
        flops=LONG,
        moved=2 * wide.size,
    )(wide)
    from_high = exchange(to_high, ("high",))
    by_chip = swap(right_sides, "chip")
    by_both = swap(by_chip, "core")
    wide = call(
        back_kernel,
        wide_shape,
        [VMEM, VMEM, VMEM],
        flops=LONG2,
        moved=4 * wide.size,
    )(from_high, wide, near_7)
    wide = exchange(wide, ("z", "chip"))
    dense, left = call(
        dense_kernel,
        [
            shape((leaves, rows, width), F32),
            shape((leaves, rows, levels * rank), BF16),
        ],
        [SMEM] + [VMEM] * 6,
        flops=LONG3,
        moved=2 * leaf_blocks.size + 12 * right_sides.size + 4 * basis_left.size,
    )(block_ranks, leaf_blocks, right_sides, by_core, by_chip, by_both, basis_left)
    coef = call(
        gather_kernel,
        shape((slots * rank, half), BF16),
        [VMEM] * 4 + [ANY],
        moved=4 * slots * rank * half,
    )(wide, near_6, near_7, near, dense)
    coef_other = swap(coef, "core")
    held = [pltpu.VMEM((leaves, rows, half), BF16), pltpu.SemaphoreType.DMA((leaves,))]
    moved = 2 * (basis_left.size + coef.size) + 4 * right_sides.size
    begun = call(
        own_kernel,
        shape((leaves, rows, width), BF16),
        [VMEM] * 3,
        scratch=held,
        whole=ANY,
        flops=flops,
        moved=moved,
    )(coef, left, dense)
    return call(
        last_kernel,
        shape((leaves, rows, width), BF16),
        [VMEM] * 3 + [ANY],
        scratch=held,
        whole=ANY,
        aliases={3: 0},
        flops=flops,
        moved=moved,
    )(coef_other, left, dense, begun)


def solution(mesh):
    clusters = mesh.shape["clus"]
    ring = 8
    fine = Mesh(
        mesh.devices.reshape(clusters // ring, ring, 2, 2), ("high", "z", "chip", "core")
    )
    places, rows = ("high", "z"), ("chip", "core")
    in_specs = (
        P(places, rows, None),
        P(places, rows, None),
        P(None, places, rows, None),
        P(None, places, rows, None),
        P(),
    )
    return jax.shard_map(
        local, mesh=fine, in_specs=in_specs, out_specs=P(places, rows, None), check_vma=False
    )
```

```python
import jax
import jax.numpy as jnp
from jax import lax
from jax.experimental import pallas as pl
from jax.experimental.pallas import tpu as pltpu
from jax.sharding import Mesh, PartitionSpec as P

VMEM_BYTES = 48 * 1024 * 1024
LONG = 20 * 10**8
LONG2 = 20 * 10**8
LONG3 = 30 * 10**8
F32 = jnp.float32
BF16 = jnp.bfloat16


def call(
    kernel, out_shape, in_specs, scratch=(), flops=0, moved=0, whole=None, aliases=None
):
    many = isinstance(out_shape, (list, tuple))
    whole = whole or VMEM
    return pl.pallas_call(
        kernel,
        out_shape=out_shape,
        in_specs=in_specs,
        out_specs=[whole] * len(out_shape) if many else whole,
        scratch_shapes=list(scratch),
        input_output_aliases=aliases or {},
        compiler_params=pltpu.CompilerParams(vmem_limit_bytes=VMEM_BYTES),
        cost_estimate=pl.CostEstimate(flops=flops, bytes_accessed=moved, transcendentals=0),
    )


SMEM = pl.BlockSpec(memory_space=pltpu.SMEM)
VMEM = pl.BlockSpec(memory_space=pltpu.VMEM)
ANY = pl.BlockSpec(memory_space=pl.ANY)


def place():
    high, chip, core = (lax.axis_index(axis) for axis in ("high", "chip", "core"))
    return lax.axis_size("z") * high + lax.axis_index("z"), core, 2 * chip + core, high


def projections( basis, sides):
    levels, leaves, rows, rank = basis.shape
    half = sides.shape[2] // 2
    both = sides[:, :, pl.ds(pl.multiple_of(place()[1] * half, half), half)]
    contract = (((0,), (0,)), ((), ()))
    for level in range(levels - 1):
        yield lax.dot_general(
            basis[level].reshape(leaves * rows, rank),
            both.reshape(leaves * rows, half),
            contract,
            preferred_element_type=F32,
        )
    for leaf in range(leaves):
        yield lax.dot_general(
            basis[levels - 1, leaf], both[leaf], contract, preferred_element_type=F32
        )


def mine_kernel(basis, sides, out):
    for slot, value in enumerate(projections(basis, sides)):
        out[slot] = value


def theirs_kernel(basis, sides, mine, wide, near):
    down, wide_levels, across = wide.shape[:3]
    for slot, value in enumerate(projections(basis, sides)):
        total = mine[slot] + value
        if slot >= wide_levels:
            near[slot - wide_levels] = total.astype(BF16)
            continue
        for col in range(across):
            part = total[:, col * 128 : (col + 1) * 128]
            wide[:, slot, col] = part.reshape(down, 8, 128).astype(BF16)


def ring_kernel(parts, out):
    high = place()[3]
    bits = out.shape[0].bit_length() - 1
    total = [None] * bits
    for level in range(bits):
        for member in range(parts.shape[0]):
            part = parts[member, level].astype(F32)
            total[level] = part if total[level] is None else total[level] + part
    out[high] = jnp.zeros(out.shape[1:], F32)
    for step in range(1, out.shape[0]):
        out[jnp.bitwise_xor(high, step)] = total[bits - step.bit_length()]


def back_kernel(high_parts, parts, near_7, out):
    high = place()[3]
    steps = high_parts.shape[0]
    bits = steps.bit_length() - 1
    members = out.shape[0]
    for level in range(bits):
        first = 1 << (bits - 1 - level)
        total = high_parts[jnp.bitwise_xor(high, first)]
        for step in range(first + 1, 2 * first):
            total = total + high_parts[jnp.bitwise_xor(high, step)]
        rounded = total.astype(BF16)
        for member in range(members):
            out[member, level] = rounded
    ring = members // 2
    for side in range(2):
        sources = [z + chip * ring for chip in range(2) for z in range(ring) if z // (ring // 2) != side]
        total = parts[sources[0], bits].astype(F32)
        for member in sources[1:]:
            total = total + parts[member, bits].astype(F32)
        rounded = total.astype(BF16)
        for member in range(members):
            if member not in sources:
                out[member, bits] = rounded


def dense_kernel(blocks, own, by_core, by_chip, by_both, out):
    leaves, rows, _ = blocks.shape
    row = place()[2]
    for leaf in range(leaves):
        total = None
        for step, sides in enumerate((own, by_core, by_chip, by_both)):
            column = pl.multiple_of(jnp.bitwise_xor(row, step) * rows, rows)
            term = jnp.dot(
                blocks[leaf, :, pl.ds(column, rows)], sides[leaf], preferred_element_type=F32
            )
            total = term if total is None else total + term
        out[leaf] = total


def gather_kernel(limits, wide, near_6, near_7, near, late, out):
    rank = wide.shape[0] * 8
    wide_levels, across = wide.shape[1:3]
    upper = wide_levels + 2
    rows = lax.broadcasted_iota(jnp.int32, (rank, 128), 0)

    def put(row, slot, parts):
        kept = rows < limits[slot, :1]
        for col, part in enumerate(parts):
            part = jnp.where(kept, part.astype(F32), 0.0).astype(BF16)
            out[row : row + rank, col * 128 : (col + 1) * 128] = part

    def halves(value):
        return [value[:, col * 128 : (col + 1) * 128] for col in range(across)]

    for level in range(wide_levels):
        parts = [wide[:, level, col].astype(F32).reshape(rank, 128) for col in range(across)]
        put((1 + level) * rank, level, parts)
    put((1 + wide_levels) * rank, wide_levels, halves(near_6[...]))
    put(upper * rank, upper - 1, halves(near_7[1]))
    put(0, upper, halves(near[3]))
    put((1 + upper) * rank, upper + 1, halves(near[2]))


def update(coef, basis, dense, column, store):
    levels, leaves, _, rank = basis.shape
    half = coef.shape[1]
    for leaf in range(leaves):
        order = list(range(levels - 1))
        order = order + [levels - 1] if leaf else [levels - 1] + order
        left = jnp.concatenate([basis[level, leaf] for level in order], axis=1)
        right = coef[leaf * rank : (leaf + levels) * rank, :]
        term = jnp.dot(left, right, preferred_element_type=F32)
        store(leaf, (dense[leaf, :, pl.ds(column, half)] + term).astype(BF16))


def own_kernel(coef, basis, dense, out, held, sems):
    half = held.shape[2]
    place_half(place()[1], coef, basis, dense, out, held, sems, half)


def last_kernel(coef, basis, dense, begun, out, held, sems):
    half = held.shape[2]
    place_half(1 - place()[1], coef, basis, dense, out, held, sems, half)


def place_half(index, coef, basis, dense, out, held, sems, half):
    column = pl.multiple_of(index * half, half)
    copies = []

    def store(leaf, value):
        held[leaf] = value
        copies.append(
            pltpu.make_async_copy(
                held.at[leaf], out.at[leaf, :, pl.ds(column, half)], sems.at[leaf]
            )
        )
        copies[-1].start()

    update(coef, basis, dense, column, store)
    for copy in copies:
        copy.wait()


def swap(block, axis, bit=1):
    return lax.ppermute(block, axis, [(i, i ^ bit) for i in range(lax.axis_size(axis))])


def local(right_sides, leaf_blocks, basis_left, basis_right, block_ranks):
    leaves, rows, width = right_sides.shape
    levels, _, _, rank = basis_left.shape
    half = width // 2
    upper = levels - 1
    ring = lax.axis_size("z")
    highs = lax.axis_size("high")
    wide_levels = levels - 3
    owners = 2 * ring
    shape = jax.ShapeDtypeStruct
    slots = upper + leaves
    tile = (half // 128, 8, 128)
    flops = 2 * levels * leaves * rows * rank * half

    def exchange(block, axes):
        flat = block.reshape((block.shape[0], -1, 128))
        moved = lax.all_to_all(flat, axes, split_axis=0, concat_axis=0, tiled=True)
        return moved.reshape(block.shape)

    position = ring * lax.axis_index("high") + lax.axis_index("z")
    heaps = [2 ** (i + 1) - 2 + jnp.right_shift(position, upper - 1 - i) for i in range(upper)]
    heaps += [2**levels - 2 + leaves * position + leaf for leaf in range(leaves)]
    chosen = jnp.stack(heaps)[:, None] == jnp.arange(block_ranks.shape[0], dtype=jnp.int32)
    limits = jnp.sum(jnp.where(chosen, block_ranks, 0), axis=1)
    limits = jnp.broadcast_to(limits[:, None, None], (slots, 8, 128))
    basis_core = swap(basis_right, "core")
    by_core = swap(right_sides, "core")
    moved = 2 * (basis_right.size + right_sides.size) + 4 * slots * rank * half
    mine = call(
        mine_kernel,
        shape((slots, rank, half), F32),
        [VMEM, VMEM],
        flops=flops,
        moved=moved,
    )(basis_right, right_sides)
    wide_shape = shape((owners, wide_levels) + tile, BF16)
    near_shape = (slots - wide_levels, rank, half)
    wide, near = call(
        theirs_kernel,
        [wide_shape, shape(near_shape, BF16)],
        [VMEM, VMEM, VMEM],
        flops=flops,
        moved=2 * moved,
    )(basis_core, by_core, mine)
    wide = exchange(wide, ("chip", "z"))
    near = (near.astype(F32) + swap(near, "chip").astype(F32)).astype(BF16)
    near_7 = swap(near[:2], "z", 1)
    near_6 = swap((near[0].astype(F32) + near_7[0].astype(F32)).astype(BF16), "z", 2)
    to_high = call(
        ring_kernel,
        shape((highs,) + tile, F32),
        [VMEM],
        flops=LONG,
        moved=2 * wide.size,
    )(wide)
    from_high = exchange(to_high, ("high",))
    by_chip = swap(right_sides, "chip")
    by_both = swap(by_chip, "core")
    wide = call(
        back_kernel,
        wide_shape,
        [VMEM, VMEM, VMEM],
        flops=LONG2,
        moved=4 * wide.size,
    )(from_high, wide, near_7)
    wide = exchange(wide, ("chip", "z"))
    dense = call(
        dense_kernel,
        shape((leaves, rows, width), F32),
        [VMEM] * 5,
        flops=LONG3,
        moved=2 * leaf_blocks.size + 12 * right_sides.size,
    )(leaf_blocks, right_sides, by_core, by_chip, by_both)
    coef = call(
        gather_kernel,
        shape((slots * rank, half), BF16),
        [VMEM] * 5 + [ANY],
        moved=4 * slots * rank * half,
    )(limits, wide, near_6, near_7, near, dense)
    coef_other = swap(coef, "core")
    held = [pltpu.VMEM((leaves, rows, half), BF16), pltpu.SemaphoreType.DMA((leaves,))]
    moved = 2 * (basis_left.size + coef.size) + 4 * right_sides.size
    begun = call(
        own_kernel,
        shape((leaves, rows, width), BF16),
        [VMEM] * 3,
        scratch=held,
        whole=ANY,
        flops=flops,
        moved=moved,
    )(coef, basis_left, dense)
    return call(
        last_kernel,
        shape((leaves, rows, width), BF16),
        [VMEM] * 3 + [ANY],
        scratch=held,
        whole=ANY,
        aliases={3: 0},
        flops=flops,
        moved=moved,
    )(coef_other, basis_left, dense, begun)


def solution(mesh):
    clusters = mesh.shape["clus"]
    ring = 8
    fine = Mesh(
        mesh.devices.reshape(clusters // ring, ring, 2, 2), ("high", "z", "chip", "core")
    )
    places, rows = ("high", "z"), ("chip", "core")
    in_specs = (
        P(places, rows, None),
        P(places, rows, None),
        P(None, places, rows, None),
        P(None, places, rows, None),
        P(),
    )
    return jax.shard_map(
        local, mesh=fine, in_specs=in_specs, out_specs=P(places, rows, None), check_vma=False
    )
```

```python
import jax
import jax.numpy as jnp
from jax import lax
from jax.experimental import pallas as pl
from jax.experimental.pallas import tpu as pltpu
from jax.sharding import Mesh, PartitionSpec as P

VMEM_BYTES = 48 * 1024 * 1024
LONG = 20 * 10**8
LONG2 = 20 * 10**8
LONG3 = 30 * 10**8
F32 = jnp.float32
BF16 = jnp.bfloat16


def call(
    kernel, out_shape, in_specs, scratch=(), flops=0, moved=0, whole=None, aliases=None
):
    many = isinstance(out_shape, (list, tuple))
    whole = whole or VMEM
    return pl.pallas_call(
        kernel,
        out_shape=out_shape,
        in_specs=in_specs,
        out_specs=[whole] * len(out_shape) if many else whole,
        scratch_shapes=list(scratch),
        input_output_aliases=aliases or {},
        compiler_params=pltpu.CompilerParams(vmem_limit_bytes=VMEM_BYTES),
        cost_estimate=pl.CostEstimate(flops=flops, bytes_accessed=moved, transcendentals=0),
    )


SMEM = pl.BlockSpec(memory_space=pltpu.SMEM)
VMEM = pl.BlockSpec(memory_space=pltpu.VMEM)
ANY = pl.BlockSpec(memory_space=pl.ANY)


def place():
    high, chip, core = (lax.axis_index(axis) for axis in (("y", "far"), "chip", "core"))
    return lax.axis_size("z") * high + lax.axis_index("z"), core, 2 * chip + core, high


def projections( basis, sides):
    levels, leaves, rows, rank = basis.shape
    half = sides.shape[2] // 2
    both = sides[:, :, pl.ds(pl.multiple_of(place()[1] * half, half), half)]
    contract = (((0,), (0,)), ((), ()))
    for level in range(levels - 1):
        yield lax.dot_general(
            basis[level].reshape(leaves * rows, rank),
            both.reshape(leaves * rows, half),
            contract,
            preferred_element_type=F32,
        )
    for leaf in range(leaves):
        yield lax.dot_general(
            basis[levels - 1, leaf], both[leaf], contract, preferred_element_type=F32
        )


def mine_kernel(basis, sides, out):
    for slot, value in enumerate(projections(basis, sides)):
        out[slot] = value


def theirs_kernel(basis, sides, mine, wide, near):
    down, wide_levels, across = wide.shape[:3]
    for slot, value in enumerate(projections(basis, sides)):
        total = mine[slot] + value
        if slot >= wide_levels:
            near[slot - wide_levels] = total.astype(BF16)
            continue
        for col in range(across):
            part = total[:, col * 128 : (col + 1) * 128]
            wide[:, slot, col] = part.reshape(down, 8, 128).astype(BF16)


def far_major(high, count):
    return (high & 1) * (count // 2) + (high >> 1)


def ring_kernel(parts, out):
    high = place()[3]
    bits = out.shape[0].bit_length() - 1
    total = [None] * bits
    for level in range(bits):
        for member in range(parts.shape[0]):
            part = parts[member, level].astype(F32)
            total[level] = part if total[level] is None else total[level] + part
    out[far_major(high, out.shape[0])] = jnp.zeros(out.shape[1:], F32)
    for step in range(1, out.shape[0]):
        out[far_major(high ^ step, out.shape[0])] = total[bits - step.bit_length()]


def back_kernel(high_parts, parts, near_7, out):
    high = place()[3]
    steps = high_parts.shape[0]
    bits = steps.bit_length() - 1
    members = out.shape[0]
    for level in range(bits):
        first = 1 << (bits - 1 - level)
        total = high_parts[far_major(high ^ first, steps)]
        for step in range(first + 1, 2 * first):
            total = total + high_parts[far_major(high ^ step, steps)]
        rounded = total.astype(BF16)
        for member in range(members):
            out[member, level] = rounded
    ring = members // 2
    for side in range(2):
        sources = [z + chip * ring for chip in range(2) for z in range(ring) if z // (ring // 2) != side]
        total = parts[sources[0], bits].astype(F32)
        for member in sources[1:]:
            total = total + parts[member, bits].astype(F32)
        rounded = total.astype(BF16)
        for member in range(members):
            if member not in sources:
                out[member, bits] = rounded


def dense_kernel(blocks, own, by_core, by_chip, by_both, out):
    leaves, rows, _ = blocks.shape
    row = place()[2]
    for leaf in range(leaves):
        total = None
        for step, sides in enumerate((own, by_core, by_chip, by_both)):
            column = pl.multiple_of(jnp.bitwise_xor(row, step) * rows, rows)
            term = jnp.dot(
                blocks[leaf, :, pl.ds(column, rows)], sides[leaf], preferred_element_type=F32
            )
            total = term if total is None else total + term
        out[leaf] = total


def gather_kernel(limits, wide, near_6, near_7, near, late, out):
    rank = wide.shape[0] * 8
    wide_levels, across = wide.shape[1:3]
    upper = wide_levels + 2
    rows = lax.broadcasted_iota(jnp.int32, (rank, 128), 0)

    def put(row, slot, parts):
        kept = rows < limits[slot, :1]
        for col, part in enumerate(parts):
            part = jnp.where(kept, part.astype(F32), 0.0).astype(BF16)
            out[row : row + rank, col * 128 : (col + 1) * 128] = part

    def halves(value):
        return [value[:, col * 128 : (col + 1) * 128] for col in range(across)]

    for level in range(wide_levels):
        parts = [wide[:, level, col].astype(F32).reshape(rank, 128) for col in range(across)]
        put((1 + level) * rank, level, parts)
    put((1 + wide_levels) * rank, wide_levels, halves(near_6[...]))
    put(upper * rank, upper - 1, halves(near_7[1]))
    put(0, upper, halves(near[3]))
    put((1 + upper) * rank, upper + 1, halves(near[2]))


def update(coef, basis, dense, column, store):
    levels, leaves, _, rank = basis.shape
    half = coef.shape[1]
    for leaf in range(leaves):
        order = list(range(levels - 1))
        order = order + [levels - 1] if leaf else [levels - 1] + order
        left = jnp.concatenate([basis[level, leaf] for level in order], axis=1)
        right = coef[leaf * rank : (leaf + levels) * rank, :]
        term = jnp.dot(left, right, preferred_element_type=F32)
        store(leaf, (dense[leaf, :, pl.ds(column, half)] + term).astype(BF16))


def own_kernel(coef, basis, dense, out, held, sems):
    half = held.shape[2]
    place_half(place()[1], coef, basis, dense, out, held, sems, half)


def last_kernel(coef, basis, dense, begun, out, held, sems):
    half = held.shape[2]
    place_half(1 - place()[1], coef, basis, dense, out, held, sems, half)


def place_half(index, coef, basis, dense, out, held, sems, half):
    column = pl.multiple_of(index * half, half)
    copies = []

    def store(leaf, value):
        held[leaf] = value
        copies.append(
            pltpu.make_async_copy(
                held.at[leaf], out.at[leaf, :, pl.ds(column, half)], sems.at[leaf]
            )
        )
        copies[-1].start()

    update(coef, basis, dense, column, store)
    for copy in copies:
        copy.wait()


def swap(block, axis, bit=1):
    return lax.ppermute(block, axis, [(i, i ^ bit) for i in range(lax.axis_size(axis))])


def local(right_sides, leaf_blocks, basis_left, basis_right, block_ranks):
    leaves, rows, width = right_sides.shape
    levels, _, _, rank = basis_left.shape
    half = width // 2
    upper = levels - 1
    ring = lax.axis_size("z")
    highs = lax.axis_size(("y", "far"))
    wide_levels = levels - 3
    owners = 2 * ring
    shape = jax.ShapeDtypeStruct
    slots = upper + leaves
    tile = (half // 128, 8, 128)
    flops = 2 * levels * leaves * rows * rank * half

    def exchange(block, axes):
        flat = block.reshape((block.shape[0], -1, 128))
        moved = lax.all_to_all(flat, axes, split_axis=0, concat_axis=0, tiled=True)
        return moved.reshape(block.shape)

    position = ring * lax.axis_index(("y", "far")) + lax.axis_index("z")
    heaps = [2 ** (i + 1) - 2 + jnp.right_shift(position, upper - 1 - i) for i in range(upper)]
    heaps += [2**levels - 2 + leaves * position + leaf for leaf in range(leaves)]
    chosen = jnp.stack(heaps)[:, None] == jnp.arange(block_ranks.shape[0], dtype=jnp.int32)
    limits = jnp.sum(jnp.where(chosen, block_ranks, 0), axis=1)
    limits = jnp.broadcast_to(limits[:, None, None], (slots, 8, 128))
    basis_core = swap(basis_right, "core")
    by_core = swap(right_sides, "core")
    moved = 2 * (basis_right.size + right_sides.size) + 4 * slots * rank * half
    mine = call(
        mine_kernel,
        shape((slots, rank, half), F32),
        [VMEM, VMEM],
        flops=flops,
        moved=moved,
    )(basis_right, right_sides)
    wide_shape = shape((owners, wide_levels) + tile, BF16)
    near_shape = (slots - wide_levels, rank, half)
    wide, near = call(
        theirs_kernel,
        [wide_shape, shape(near_shape, BF16)],
        [VMEM, VMEM, VMEM],
        flops=flops,
        moved=2 * moved,
    )(basis_core, by_core, mine)
    wide = exchange(wide, ("chip", "z"))
    near = (near.astype(F32) + swap(near, "chip").astype(F32)).astype(BF16)
    near_7 = swap(near[:2], "z", 1)
    near_6 = swap((near[0].astype(F32) + near_7[0].astype(F32)).astype(BF16), "z", 2)
    to_high = call(
        ring_kernel,
        shape((highs,) + tile, F32),
        [VMEM],
        flops=LONG,
        moved=2 * wide.size,
    )(wide)
    from_high = exchange(to_high, ("far", "y"))
    by_chip = swap(right_sides, "chip")
    by_both = swap(by_chip, "core")
    wide = call(
        back_kernel,
        wide_shape,
        [VMEM, VMEM, VMEM],
        flops=LONG2,
        moved=4 * wide.size,
    )(from_high, wide, near_7)
    wide = exchange(wide, ("chip", "z"))
    dense = call(
        dense_kernel,
        shape((leaves, rows, width), F32),
        [VMEM] * 5,
        flops=LONG3,
        moved=2 * leaf_blocks.size + 12 * right_sides.size,
    )(leaf_blocks, right_sides, by_core, by_chip, by_both)
    coef = call(
        gather_kernel,
        shape((slots * rank, half), BF16),
        [VMEM] * 5 + [ANY],
        moved=4 * slots * rank * half,
    )(limits, wide, near_6, near_7, near, dense)
    coef_other = swap(coef, "core")
    held = [pltpu.VMEM((leaves, rows, half), BF16), pltpu.SemaphoreType.DMA((leaves,))]
    moved = 2 * (basis_left.size + coef.size) + 4 * right_sides.size
    begun = call(
        own_kernel,
        shape((leaves, rows, width), BF16),
        [VMEM] * 3,
        scratch=held,
        whole=ANY,
        flops=flops,
        moved=moved,
    )(coef, basis_left, dense)
    return call(
        last_kernel,
        shape((leaves, rows, width), BF16),
        [VMEM] * 3 + [ANY],
        scratch=held,
        whole=ANY,
        aliases={3: 0},
        flops=flops,
        moved=moved,
    )(coef_other, basis_left, dense, begun)


def solution(mesh):
    clusters = mesh.shape["clus"]
    ring = 8
    fine = Mesh(
        mesh.devices.reshape(clusters // (2 * ring), 2, ring, 2, 2),
        ("y", "far", "z", "chip", "core"),
    )
    places, rows = ("y", "far", "z"), ("chip", "core")
    in_specs = (
        P(places, rows, None),
        P(places, rows, None),
        P(None, places, rows, None),
        P(None, places, rows, None),
        P(),
    )
    return jax.shard_map(
        local, mesh=fine, in_specs=in_specs, out_specs=P(places, rows, None), check_vma=False
    )
```

```python
import jax
import jax.numpy as jnp
from jax import lax
from jax.experimental import pallas as pl
from jax.experimental.pallas import tpu as pltpu
from jax.sharding import Mesh, PartitionSpec as P

VMEM_BYTES = 48 * 1024 * 1024
LONG = 20 * 10**8
LONG2 = 20 * 10**8
LONG3 = 30 * 10**8
F32 = jnp.float32
BF16 = jnp.bfloat16


def call(
    kernel, out_shape, in_specs, scratch=(), flops=0, moved=0, whole=None, aliases=None
):
    many = isinstance(out_shape, (list, tuple))
    whole = whole or VMEM
    return pl.pallas_call(
        kernel,
        out_shape=out_shape,
        in_specs=in_specs,
        out_specs=[whole] * len(out_shape) if many and not isinstance(whole, list) else whole,
        scratch_shapes=list(scratch),
        input_output_aliases=aliases or {},
        compiler_params=pltpu.CompilerParams(vmem_limit_bytes=VMEM_BYTES),
        cost_estimate=pl.CostEstimate(flops=flops, bytes_accessed=moved, transcendentals=0),
    )


SMEM = pl.BlockSpec(memory_space=pltpu.SMEM)
VMEM = pl.BlockSpec(memory_space=pltpu.VMEM)
ANY = pl.BlockSpec(memory_space=pl.ANY)


def place():
    high, chip, core = (lax.axis_index(axis) for axis in (("y", "far"), "chip", "core"))
    return lax.axis_size("z") * high + lax.axis_index("z"), core, 2 * chip + core, high


def projections( basis, sides):
    levels, leaves, rows, rank = basis.shape
    half = sides.shape[2] // 2
    both = sides[:, :, pl.ds(pl.multiple_of(place()[1] * half, half), half)]
    contract = (((0,), (0,)), ((), ()))
    for level in range(levels - 1):
        yield lax.dot_general(
            basis[level].reshape(leaves * rows, rank),
            both.reshape(leaves * rows, half),
            contract,
            preferred_element_type=F32,
        )
    for leaf in range(leaves):
        yield lax.dot_general(
            basis[levels - 1, leaf], both[leaf], contract, preferred_element_type=F32
        )


def mine_kernel(basis, sides, out):
    for slot, value in enumerate(projections(basis, sides)):
        out[slot] = value


def theirs_kernel(basis, sides, mine, wide, near, tiles, sems):
    down, wide_levels, across = wide.shape[:3]
    copies = []
    for slot, value in enumerate(projections(basis, sides)):
        total = mine[slot] + value
        if slot >= wide_levels:
            near[slot - wide_levels] = total.astype(BF16)
            continue
        for col in range(across):
            part = total[:, col * 128 : (col + 1) * 128]
            tiles[slot, :, col] = part.reshape(down, 8, 128).astype(BF16)
        copies.append(pltpu.make_async_copy(tiles.at[slot], wide.at[:, slot], sems.at[slot]))
        copies[-1].start()
    for copy in copies:
        copy.wait()


def far_major(high, count):
    return (high & 1) * (count // 2) + (high >> 1)


def ring_kernel(parts, out):
    high = place()[3]
    bits = out.shape[0].bit_length() - 1
    total = [None] * bits
    for level in range(bits):
        for member in range(parts.shape[0]):
            part = parts[member, level].astype(F32)
            total[level] = part if total[level] is None else total[level] + part
    out[far_major(high, out.shape[0])] = jnp.zeros(out.shape[1:], F32)
    for step in range(1, out.shape[0]):
        out[far_major(high ^ step, out.shape[0])] = total[bits - step.bit_length()]


def back_kernel(high_parts, parts, near_7, out):
    high = place()[3]
    steps = high_parts.shape[0]
    bits = steps.bit_length() - 1
    members = out.shape[0]
    for level in range(bits):
        first = 1 << (bits - 1 - level)
        total = high_parts[far_major(high ^ first, steps)]
        for step in range(first + 1, 2 * first):
            total = total + high_parts[far_major(high ^ step, steps)]
        rounded = total.astype(BF16)
        for member in range(members):
            out[member, level] = rounded
    ring = members // 2
    for side in range(2):
        sources = [z + chip * ring for chip in range(2) for z in range(ring) if z // (ring // 2) != side]
        total = parts[sources[0], bits].astype(F32)
        for member in sources[1:]:
            total = total + parts[member, bits].astype(F32)
        rounded = total.astype(BF16)
        for member in range(members):
            if member not in sources:
                out[member, bits] = rounded


def dense_kernel(blocks, own, by_core, by_chip, by_both, out):
    leaves, rows, _ = blocks.shape
    row = place()[2]
    for leaf in range(leaves):
        total = None
        for step, sides in enumerate((own, by_core, by_chip, by_both)):
            column = pl.multiple_of(jnp.bitwise_xor(row, step) * rows, rows)
            term = jnp.dot(
                blocks[leaf, :, pl.ds(column, rows)], sides[leaf], preferred_element_type=F32
            )
            total = term if total is None else total + term
        out[leaf] = total


def gather_kernel(limits, wide, near_6, near_7, near, late, out):
    rank = wide.shape[0] * 8
    wide_levels, across = wide.shape[1:3]
    upper = wide_levels + 2
    rows = lax.broadcasted_iota(jnp.int32, (rank, 128), 0)

    def put(row, slot, parts):
        kept = rows < limits[slot, :1]
        for col, part in enumerate(parts):
            part = jnp.where(kept, part.astype(F32), 0.0).astype(BF16)
            out[row : row + rank, col * 128 : (col + 1) * 128] = part

    def halves(value):
        return [value[:, col * 128 : (col + 1) * 128] for col in range(across)]

    for level in range(wide_levels):
        parts = [wide[:, level, col].astype(F32).reshape(rank, 128) for col in range(across)]
        put(level * rank, level, parts)
    put(wide_levels * rank, wide_levels, halves(near_6[...]))
    put(upper * rank, upper - 1, halves(near_7[1]))
    put((upper - 1) * rank, upper, halves(near[3]))
    put((upper + 1) * rank, upper + 1, halves(near[2]))


def update(coef, basis, dense, column, store):
    levels, leaves, rows, rank = basis.shape
    half = coef.shape[1]
    shared = levels - 2
    left = jnp.concatenate(
        [basis[level].reshape(leaves * rows, rank) for level in range(shared)], axis=1
    )
    both = jnp.dot(left, coef[: shared * rank, :], preferred_element_type=F32)
    for leaf in range(leaves):
        order = (levels - 2, levels - 1) if leaf else (levels - 1, levels - 2)
        left = jnp.concatenate([basis[level, leaf] for level in order], axis=1)
        right = coef[(shared + leaf) * rank : (shared + leaf + 2) * rank, :]
        term = jnp.dot(left, right, preferred_element_type=F32)
        term = term + both[leaf * rows : (leaf + 1) * rows]
        store(leaf, (dense[leaf, :, pl.ds(column, half)] + term).astype(BF16))


def own_kernel(coef, basis, dense, out, held, sems):
    half = held.shape[2]
    place_half(place()[1], coef, basis, dense, out, held, sems, half)


def last_kernel(coef, basis, dense, begun, out, held, sems):
    half = held.shape[2]
    place_half(1 - place()[1], coef, basis, dense, out, held, sems, half)


def place_half(index, coef, basis, dense, out, held, sems, half):
    column = pl.multiple_of(index * half, half)
    copies = []

    def store(leaf, value):
        held[leaf] = value
        copies.append(
            pltpu.make_async_copy(
                held.at[leaf], out.at[leaf, :, pl.ds(column, half)], sems.at[leaf]
            )
        )
        copies[-1].start()

    update(coef, basis, dense, column, store)
    for copy in copies:
        copy.wait()


def swap(block, axis, bit=1):
    return lax.ppermute(block, axis, [(i, i ^ bit) for i in range(lax.axis_size(axis))])


def local(right_sides, leaf_blocks, basis_left, basis_right, block_ranks):
    leaves, rows, width = right_sides.shape
    levels, _, _, rank = basis_left.shape
    half = width // 2
    upper = levels - 1
    ring = lax.axis_size("z")
    highs = lax.axis_size(("y", "far"))
    wide_levels = levels - 3
    owners = 2 * ring
    shape = jax.ShapeDtypeStruct
    slots = upper + leaves
    tile = (half // 128, 8, 128)
    flops = 2 * levels * leaves * rows * rank * half

    def exchange(block, axes):
        flat = block.reshape((block.shape[0], -1, 128))
        moved = lax.all_to_all(flat, axes, split_axis=0, concat_axis=0, tiled=True)
        return moved.reshape(block.shape)

    position = ring * lax.axis_index(("y", "far")) + lax.axis_index("z")
    heaps = [2 ** (i + 1) - 2 + jnp.right_shift(position, upper - 1 - i) for i in range(upper)]
    heaps += [2**levels - 2 + leaves * position + leaf for leaf in range(leaves)]
    chosen = jnp.stack(heaps)[:, None] == jnp.arange(block_ranks.shape[0], dtype=jnp.int32)
    limits = jnp.sum(jnp.where(chosen, block_ranks, 0), axis=1)
    limits = jnp.broadcast_to(limits[:, None, None], (slots, 8, 128))
    basis_core = swap(basis_right, "core")
    by_core = swap(right_sides, "core")
    moved = 2 * (basis_right.size + right_sides.size) + 4 * slots * rank * half
    mine = call(
        mine_kernel,
        shape((slots, rank, half), F32),
        [VMEM, VMEM],
        flops=flops,
        moved=moved,
    )(basis_right, right_sides)
    wide_shape = shape((owners, wide_levels) + tile, BF16)
    near_shape = (slots - wide_levels, rank, half)
    wide, near = call(
        theirs_kernel,
        [wide_shape, shape(near_shape, BF16)],
        [VMEM, VMEM, VMEM],
        scratch=[
            pltpu.VMEM((wide_levels, owners) + tile, BF16),
            pltpu.SemaphoreType.DMA((wide_levels,)),
        ],
        whole=[ANY, VMEM],
        flops=flops,
        moved=2 * moved,
    )(basis_core, by_core, mine)
    wide = exchange(wide, ("chip", "z"))
    near = (near.astype(F32) + swap(near, "chip").astype(F32)).astype(BF16)
    near_7 = swap(near[:2], "z", 1)
    near_6 = swap((near[0].astype(F32) + near_7[0].astype(F32)).astype(BF16), "z", 2)
    to_high = call(
        ring_kernel,
        shape((highs,) + tile, F32),
        [VMEM],
        flops=LONG,
        moved=2 * wide.size,
    )(wide)
    from_high = exchange(to_high, ("far", "y"))
    by_chip = swap(right_sides, "chip")
    by_both = swap(by_chip, "core")
    wide = call(
        back_kernel,
        wide_shape,
        [VMEM, VMEM, VMEM],
        flops=LONG2,
        moved=4 * wide.size,
    )(from_high, wide, near_7)
    wide = exchange(wide, ("chip", "z"))
    dense = call(
        dense_kernel,
        shape((leaves, rows, width), F32),
        [VMEM] * 5,
        flops=LONG3,
        moved=2 * leaf_blocks.size + 12 * right_sides.size,
    )(leaf_blocks, right_sides, by_core, by_chip, by_both)
    coef = call(
        gather_kernel,
        shape((slots * rank, half), BF16),
        [VMEM] * 5 + [ANY],
        moved=4 * slots * rank * half,
    )(limits, wide, near_6, near_7, near, dense)
    coef_other = swap(coef, "core")
    held = [pltpu.VMEM((leaves, rows, half), BF16), pltpu.SemaphoreType.DMA((leaves,))]
    moved = 2 * (basis_left.size + coef.size) + 4 * right_sides.size
    begun = call(
        own_kernel,
        shape((leaves, rows, width), BF16),
        [VMEM] * 3,
        scratch=held,
        whole=ANY,
        flops=flops,
        moved=moved,
    )(coef, basis_left, dense)
    return call(
        last_kernel,
        shape((leaves, rows, width), BF16),
        [VMEM] * 3 + [ANY],
        scratch=held,
        whole=ANY,
        aliases={3: 0},
        flops=flops,
        moved=moved,
    )(coef_other, basis_left, dense, begun)


def solution(mesh):
    clusters = mesh.shape["clus"]
    ring = 8
    fine = Mesh(
        mesh.devices.reshape(clusters // (2 * ring), 2, ring, 2, 2),
        ("y", "far", "z", "chip", "core"),
    )
    places, rows = ("y", "far", "z"), ("chip", "core")
    in_specs = (
        P(places, rows, None),
        P(places, rows, None),
        P(None, places, rows, None),
        P(None, places, rows, None),
        P(),
    )
    return jax.shard_map(
        local, mesh=fine, in_specs=in_specs, out_specs=P(places, rows, None), check_vma=False
    )
```

```python
import jax
import jax.numpy as jnp
from jax import lax
from jax.experimental import pallas as pl
from jax.experimental.pallas import tpu as pltpu
from jax.sharding import Mesh, PartitionSpec as P

VMEM_BYTES = 48 * 1024 * 1024
LONG = 20 * 10**8
LONG2 = 20 * 10**8
LONG3 = 30 * 10**8
F32 = jnp.float32
BF16 = jnp.bfloat16


def call(
    kernel, out_shape, in_specs, scratch=(), flops=0, moved=0, whole=None, aliases=None
):
    many = isinstance(out_shape, (list, tuple))
    whole = whole or VMEM
    return pl.pallas_call(
        kernel,
        out_shape=out_shape,
        in_specs=in_specs,
        out_specs=[whole] * len(out_shape) if many else whole,
        scratch_shapes=list(scratch),
        input_output_aliases=aliases or {},
        compiler_params=pltpu.CompilerParams(vmem_limit_bytes=VMEM_BYTES),
        cost_estimate=pl.CostEstimate(flops=flops, bytes_accessed=moved, transcendentals=0),
    )


SMEM = pl.BlockSpec(memory_space=pltpu.SMEM)
VMEM = pl.BlockSpec(memory_space=pltpu.VMEM)
ANY = pl.BlockSpec(memory_space=pl.ANY)


def place():
    high, chip, core = (lax.axis_index(axis) for axis in (("y", "far"), "chip", "core"))
    return lax.axis_size("z") * high + lax.axis_index("z"), core, 2 * chip + core, high


def projections( basis, sides):
    levels, leaves, rows, rank = basis.shape
    half = sides.shape[2] // 2
    both = sides[:, :, pl.ds(pl.multiple_of(place()[1] * half, half), half)]
    contract = (((0,), (0,)), ((), ()))
    for level in range(levels - 1):
        yield lax.dot_general(
            basis[level].reshape(leaves * rows, rank),
            both.reshape(leaves * rows, half),
            contract,
            preferred_element_type=F32,
        )
    for leaf in range(leaves):
        yield lax.dot_general(
            basis[levels - 1, leaf], both[leaf], contract, preferred_element_type=F32
        )


def mine_kernel(basis, sides, out):
    for slot, value in enumerate(projections(basis, sides)):
        out[slot] = value


def theirs_kernel(basis, sides, mine, wide, near):
    down, wide_levels, across = wide.shape[:3]
    for slot, value in enumerate(projections(basis, sides)):
        total = mine[slot] + value
        if slot >= wide_levels:
            near[slot - wide_levels] = total.astype(BF16)
            continue
        for col in range(across):
            part = total[:, col * 128 : (col + 1) * 128]
            wide[:, slot, col] = part.reshape(down, 8, 128).astype(BF16)


def far_major(high, count):
    return (high & 1) * (count // 2) + (high >> 1)


def near_kernel(mine, theirs, late, out):
    out[...] = (mine[...].astype(F32) + theirs[...].astype(F32)).astype(BF16)


def ring_kernel(parts, out):
    high = place()[3]
    bits = out.shape[0].bit_length() - 1
    total = [None] * bits
    for level in range(bits):
        for member in range(parts.shape[0]):
            part = parts[member, level].astype(F32)
            total[level] = part if total[level] is None else total[level] + part
    out[far_major(high, out.shape[0])] = jnp.zeros(out.shape[1:], F32)
    for step in range(1, out.shape[0]):
        out[far_major(high ^ step, out.shape[0])] = total[bits - step.bit_length()]


def back_kernel(high_parts, parts, near_7, out):
    high = place()[3]
    steps = high_parts.shape[0]
    bits = steps.bit_length() - 1
    members = out.shape[0]
    for level in range(bits):
        first = 1 << (bits - 1 - level)
        total = high_parts[far_major(high ^ first, steps)]
        for step in range(first + 1, 2 * first):
            total = total + high_parts[far_major(high ^ step, steps)]
        rounded = total.astype(BF16)
        for member in range(members):
            out[member, level] = rounded
    ring = members // 2
    for side in range(2):
        sources = [z + chip * ring for chip in range(2) for z in range(ring) if z // (ring // 2) != side]
        total = parts[sources[0], bits].astype(F32)
        for member in sources[1:]:
            total = total + parts[member, bits].astype(F32)
        rounded = total.astype(BF16)
        for member in range(members):
            if member not in sources:
                out[member, bits] = rounded


def dense_kernel(blocks, own, by_core, by_chip, by_both, out):
    leaves, rows, _ = blocks.shape
    row = place()[2]
    for leaf in range(leaves):
        total = None
        for step, sides in enumerate((own, by_core, by_chip, by_both)):
            column = pl.multiple_of(jnp.bitwise_xor(row, step) * rows, rows)
            term = jnp.dot(
                blocks[leaf, :, pl.ds(column, rows)], sides[leaf], preferred_element_type=F32
            )
            total = term if total is None else total + term
        out[leaf] = total


def gather_kernel(limits, wide, near_6, near_7, near, late, out):
    rank = wide.shape[0] * 8
    wide_levels, across = wide.shape[1:3]
    upper = wide_levels + 2
    rows = lax.broadcasted_iota(jnp.int32, (rank, 128), 0)

    def put(row, slot, parts):
        kept = rows < limits[slot, :1]
        for col, part in enumerate(parts):
            part = jnp.where(kept, part.astype(F32), 0.0).astype(BF16)
            out[row : row + rank, col * 128 : (col + 1) * 128] = part

    def halves(value):
        return [value[:, col * 128 : (col + 1) * 128] for col in range(across)]

    for level in range(wide_levels):
        parts = [wide[:, level, col].astype(F32).reshape(rank, 128) for col in range(across)]
        put((1 + level) * rank, level, parts)
    put((1 + wide_levels) * rank, wide_levels, halves(near_6[...]))
    put(upper * rank, upper - 1, halves(near_7[1]))
    put(0, upper, halves(near[3]))
    put((1 + upper) * rank, upper + 1, halves(near[2]))


def update(coef, basis, dense, column, store):
    levels, leaves, _, rank = basis.shape
    half = coef.shape[1]
    for leaf in range(leaves):
        order = list(range(levels - 1))
        order = order + [levels - 1] if leaf else [levels - 1] + order
        left = jnp.concatenate([basis[level, leaf] for level in order], axis=1)
        right = coef[leaf * rank : (leaf + levels) * rank, :]
        term = jnp.dot(left, right, preferred_element_type=F32)
        store(leaf, (dense[leaf, :, pl.ds(column, half)] + term).astype(BF16))


def own_kernel(coef, basis, dense, out, held, sems):
    half = held.shape[2]
    place_half(place()[1], coef, basis, dense, out, held, sems, half)


def last_kernel(coef, basis, dense, begun, out, held, sems):
    half = held.shape[2]
    place_half(1 - place()[1], coef, basis, dense, out, held, sems, half)


def place_half(index, coef, basis, dense, out, held, sems, half):
    column = pl.multiple_of(index * half, half)
    copies = []

    def store(leaf, value):
        held[leaf] = value
        copies.append(
            pltpu.make_async_copy(
                held.at[leaf], out.at[leaf, :, pl.ds(column, half)], sems.at[leaf]
            )
        )
        copies[-1].start()

    update(coef, basis, dense, column, store)
    for copy in copies:
        copy.wait()


def swap(block, axis, bit=1):
    return lax.ppermute(block, axis, [(i, i ^ bit) for i in range(lax.axis_size(axis))])


def local(right_sides, leaf_blocks, basis_left, basis_right, block_ranks):
    leaves, rows, width = right_sides.shape
    levels, _, _, rank = basis_left.shape
    half = width // 2
    upper = levels - 1
    ring = lax.axis_size("z")
    highs = lax.axis_size(("y", "far"))
    wide_levels = levels - 3
    owners = 2 * ring
    shape = jax.ShapeDtypeStruct
    slots = upper + leaves
    tile = (half // 128, 8, 128)
    flops = 2 * levels * leaves * rows * rank * half

    def exchange(block, axes):
        flat = block.reshape((block.shape[0], -1, 128))
        moved = lax.all_to_all(flat, axes, split_axis=0, concat_axis=0, tiled=True)
        return moved.reshape(block.shape)

    position = ring * lax.axis_index(("y", "far")) + lax.axis_index("z")
    heaps = [2 ** (i + 1) - 2 + jnp.right_shift(position, upper - 1 - i) for i in range(upper)]
    heaps += [2**levels - 2 + leaves * position + leaf for leaf in range(leaves)]
    chosen = jnp.stack(heaps)[:, None] == jnp.arange(block_ranks.shape[0], dtype=jnp.int32)
    limits = jnp.sum(jnp.where(chosen, block_ranks, 0), axis=1)
    limits = jnp.broadcast_to(limits[:, None, None], (slots, 8, 128))
    basis_core = swap(basis_right, "core")
    by_core = swap(right_sides, "core")
    moved = 2 * (basis_right.size + right_sides.size) + 4 * slots * rank * half
    mine = call(
        mine_kernel,
        shape((slots, rank, half), F32),
        [VMEM, VMEM],
        flops=flops,
        moved=moved,
    )(basis_right, right_sides)
    wide_shape = shape((owners, wide_levels) + tile, BF16)
    near_shape = (slots - wide_levels, rank, half)
    wide, near = call(
        theirs_kernel,
        [wide_shape, shape(near_shape, BF16)],
        [VMEM, VMEM, VMEM],
        flops=flops,
        moved=2 * moved,
    )(basis_core, by_core, mine)
    wide = exchange(wide, ("chip", "z"))
    near = call(
        near_kernel, shape(near_shape, BF16), [VMEM, VMEM, ANY], moved=6 * slots * rank * half
    )(near, swap(near, "chip"), wide)
    near_7 = swap(near[:2], "z", 1)
    near_6 = swap((near[0].astype(F32) + near_7[0].astype(F32)).astype(BF16), "z", 2)
    to_high = call(
        ring_kernel,
        shape((highs,) + tile, F32),
        [VMEM],
        flops=LONG,
        moved=2 * wide.size,
    )(wide)
    from_high = exchange(to_high, ("far", "y"))
    by_chip = swap(right_sides, "chip")
    by_both = swap(by_chip, "core")
    wide = call(
        back_kernel,
        wide_shape,
        [VMEM, VMEM, VMEM],
        flops=LONG2,
        moved=4 * wide.size,
    )(from_high, wide, near_7)
    wide = exchange(wide, ("chip", "z"))
    dense = call(
        dense_kernel,
        shape((leaves, rows, width), F32),
        [VMEM] * 5,
        flops=LONG3,
        moved=2 * leaf_blocks.size + 12 * right_sides.size,
    )(leaf_blocks, right_sides, by_core, by_chip, by_both)
    coef = call(
        gather_kernel,
        shape((slots * rank, half), BF16),
        [VMEM] * 5 + [ANY],
        moved=4 * slots * rank * half,
    )(limits, wide, near_6, near_7, near, dense)
    coef_other = swap(coef, "core")
    held = [pltpu.VMEM((leaves, rows, half), BF16), pltpu.SemaphoreType.DMA((leaves,))]
    moved = 2 * (basis_left.size + coef.size) + 4 * right_sides.size
    begun = call(
        own_kernel,
        shape((leaves, rows, width), BF16),
        [VMEM] * 3,
        scratch=held,
        whole=ANY,
        flops=flops,
        moved=moved,
    )(coef, basis_left, dense)
    return call(
        last_kernel,
        shape((leaves, rows, width), BF16),
        [VMEM] * 3 + [ANY],
        scratch=held,
        whole=ANY,
        aliases={3: 0},
        flops=flops,
        moved=moved,
    )(coef_other, basis_left, dense, begun)


def solution(mesh):
    clusters = mesh.shape["clus"]
    ring = 8
    fine = Mesh(
        mesh.devices.reshape(clusters // (2 * ring), 2, ring, 2, 2),
        ("y", "far", "z", "chip", "core"),
    )
    places, rows = ("y", "far", "z"), ("chip", "core")
    in_specs = (
        P(places, rows, None),
        P(places, rows, None),
        P(None, places, rows, None),
        P(None, places, rows, None),
        P(),
    )
    return jax.shard_map(
        local, mesh=fine, in_specs=in_specs, out_specs=P(places, rows, None), check_vma=False
    )
```
